32 devices in a mesh: half: 2 (over core), dom: 8 (over z, y), slab: 2 (over x).
Axes of the slice: x: 2, y: 2, z: 4, core: 2. Of those that a mesh axis runs over, the one named last changes fastest.
Arguments:
- volume: float32 [2, 2048, 400], P('half', 'slab')
- images: bfloat16 [2, 8192, 400], P('half', 'dom'), may hold values from -18 to 18
- tap_index: int32 [2, 2, 8, 8192], P('half', 'slab', None, 'dom'), may hold values from 0 to 1023, as said below
- tap_weight: float32 [2, 2, 8, 8192], P('half', 'slab', None, 'dom'), may hold values from 0.2 to 1
- classes: int32 [2, 128], P('half', 'dom'), may hold values from 0 to 15
- shifts: int32 [2, 2, 128], P('half', None, 'dom'), may hold values from -8 to 8
- defocus: float32 [16], replicated, may hold values from 0.5 to 3
Outputs:
- updated: float32 [2, 2048, 400], P('half', 'slab')
The draws below stay inside these ranges and needn't reach their ends.
Inputs may be any that keep to these rules, and one draw needn't show every extreme that they name: `tap_index`: the 8 taps of one line and slab read 8 consecutive map lines.
All inputs are finite; a program needn't handle non-finite values.
Results may differ from the reference program's by a relative error of at most 0.0035.
Values may be sent and summed in bfloat16 or wider, within the bound.
A program may use at most 64 MiB of HBM per device.

```python
import math
import jax
import jax.numpy as jnp
from jax import lax

R = 200
LPI = 64
K = 8
CLASSES = 16
LINES_SLAB = 1024
P_DEV = 16
PARTICLES = 128
ROWS = 8192
LINES = 2048
N_DOM = 8
N_SLAB = 2


def draw_volume(key, part):
    key_shared, key_own, key_mix = jax.random.split(key, 3)
    shared = jax.random.normal(key_shared, (1, LINES, 2 * R), jnp.float32)
    own = jax.random.normal(key_own, (2, LINES, 2 * R), jnp.float32)
    mixing = jax.random.uniform(key_mix, (R,), jnp.float32, 0.0, 0.9)
    columns = jnp.concatenate([mixing, mixing])[None, None, :]
    return jnp.sqrt(columns) * shared + jnp.sqrt(1.0 - columns) * own


def draw_tap_index(key, part):
    base = jax.random.randint(key, (2, N_SLAB, 1, ROWS), 0, LINES_SLAB - K + 1)
    return base + jnp.arange(K, dtype=jnp.int32)[None, None, :, None]


def plant(drawn, key, least, largest):
    longest = drawn.shape.index(max(drawn.shape))
    spots = []
    for shift in (0, 1):
        where = [jax.random.randint(jax.random.fold_in(key, axis), (), 0, length) for axis, length in enumerate(drawn.shape)]
        where[longest] = (where[longest] + shift) % drawn.shape[longest]
        spots.append(tuple(where))
    return drawn.at[spots[0]].set(least).at[spots[1]].set(largest)


def shard_levels(key, extent, cuts, least, largest):
    factor_of = 1.0
    for position, shards_of in cuts:
        draws = jax.random.uniform(jax.random.fold_in(jax.random.fold_in(key, 6), position), (shards_of,), jnp.float32, least / len(cuts), largest / len(cuts))
        factor_of = factor_of * jnp.repeat(jnp.exp(draws), extent[position] // shards_of).reshape((-1,) + (1,) * (len(extent) - 1 - position))
    return factor_of


def normal_values(rng, extent, scale, bound, shards=(), kind=jnp.bfloat16):
    values = jax.random.normal(rng, extent, jnp.float32) * scale
    if len(shards) > 0:
        values = shard_levels(rng, extent, shards, -0.22, 0.18) * values
    return jnp.clip(values, min=-bound, max=bound).astype(kind)


def setup_inputs(seed: int = 0) -> dict:
    streams_of = jax.random.split(jax.random.key(seed), 8)
    volume = draw_volume(jax.random.fold_in(streams_of[7], 71), 0)
    images = normal_values(streams_of[1], (2, ROWS, 2 * R), 3.0, 18.0, ((0, 2), (1, 8)))
    tap_index = draw_tap_index(jax.random.fold_in(streams_of[7], 71), 0)
    tap_weight = jnp.clip(0.2 + 0.8 * jax.random.uniform(streams_of[3], (2, N_SLAB, K, ROWS), jnp.float32) ** shard_levels(streams_of[3], (2, N_SLAB, K, ROWS), ((0, 2), (1, 2), (3, 8)), -0.2, 0.2), 0.2, 1.0)
    classes = plant(jax.random.randint(streams_of[4], (2, PARTICLES), 0, CLASSES), jax.random.fold_in(streams_of[4], 1), 0, CLASSES - 1).astype(jnp.int32)
    shifts = plant(jax.random.randint(streams_of[5], (2, 2, PARTICLES), -8, 9), jax.random.fold_in(streams_of[5], 1), -8, 8).astype(jnp.int32)
    defocus = jnp.clip(jnp.exp(jax.random.uniform(streams_of[6], (CLASSES,), jnp.float32, math.log(0.5), math.log(3.0))), 0.5, 3.0)
    return {"volume": volume, "images": images, "tap_index": tap_index, "tap_weight": tap_weight, "classes": classes, "shifts": shifts, "defocus": defocus}


CTF_GAIN = 30.0
PHASE_ZERO = 0.1
STEP_SCALE = 0.5

def line_terms(classes_half, shifts_half, defocus):
    radius = jnp.arange(R, dtype=jnp.float32)
    focus = defocus[classes_half]
    ctf_part = -jnp.sin(CTF_GAIN * focus[:, None] * (radius[None, :] / R) ** 2 + PHASE_ZERO)
    ctf_rows = jnp.repeat(ctf_part, LPI, axis=0)
    theta = jnp.pi * jnp.arange(LPI, dtype=jnp.float32) / LPI
    theta_rows = jnp.tile(theta, classes_half.shape[0])
    shift_x = jnp.repeat(shifts_half[0].astype(jnp.float32), LPI)
    shift_y = jnp.repeat(shifts_half[1].astype(jnp.float32), LPI)
    along = shift_x * jnp.cos(theta_rows) + shift_y * jnp.sin(theta_rows)
    phase = 2.0 * jnp.pi * radius[None, :] * along[:, None] / (2.0 * R)
    return (ctf_rows, jnp.cos(phase), jnp.sin(phase))

def reference(volume, images, tap_index, tap_weight, classes, shifts, defocus):
    step = STEP_SCALE / math.sqrt(P_DEV * LPI * N_DOM * K / LINES_SLAB)
    grads = []
    cands = []
    for half_num in range(2):
        map_low = volume[half_num].astype(jnp.bfloat16)
        weights = tap_weight[half_num].astype(jnp.bfloat16).astype(jnp.float32)
        proj = jnp.zeros((ROWS, 2 * R), jnp.float32)
        for slab_num in range(N_SLAB):
            partial_value = jnp.zeros((ROWS, 2 * R), jnp.float32)
            for tap_num in range(K):
                lines = map_low[slab_num * LINES_SLAB + tap_index[half_num, slab_num, tap_num]]
                partial_value = partial_value + weights[slab_num, tap_num][:, None] * lines.astype(jnp.float32)
            proj = proj + partial_value
        ctf_rows, cosine, sine_part = line_terms(classes[half_num], shifts[half_num], defocus)
        proj_re, proj_im = (proj[:, :R], proj[:, R:])
        data = images[half_num].astype(jnp.float32)
        res_re = ctf_rows * (cosine * proj_re - sine_part * proj_im) - data[:, :R]
        res_im = ctf_rows * (sine_part * proj_re + cosine * proj_im) - data[:, R:]
        back_re = ctf_rows * (cosine * res_re + sine_part * res_im)
        back_im = ctf_rows * (cosine * res_im - sine_part * res_re)
        back = jnp.concatenate([back_re, back_im], axis=1).astype(jnp.bfloat16).astype(jnp.float32)
        pieces = []
        for slab_num in range(N_SLAB):
            piece = jnp.zeros((LINES_SLAB, 2 * R), jnp.float32)
            for tap_num in range(K):
                piece = piece.at[tap_index[half_num, slab_num, tap_num]].add(weights[slab_num, tap_num][:, None] * back)
            pieces.append(piece)
        grad = jnp.concatenate(pieces, axis=0)
        grads.append(grad)
        cands.append(volume[half_num] - step * grad)
    first, second = cands
    num = lax.optimization_barrier(jnp.sum(first[:, :R] * second[:, :R] + first[:, R:] * second[:, R:], axis=0))
    den_first = lax.optimization_barrier(jnp.sum(first[:, :R] ** 2 + first[:, R:] ** 2, axis=0))
    den_second = lax.optimization_barrier(jnp.sum(second[:, :R] ** 2 + second[:, R:] ** 2, axis=0))
    fsc = num / (jnp.sqrt(den_first * den_second) + 1e-06)
    factor = jnp.tile((1.0 + fsc) / 2.0, 2)
    outs = [volume[half_num] - step * factor[None, :] * grads[half_num] for half_num in range(2)]
    return jnp.stack(outs, axis=0)
```

```python
import functools
import math

import jax
import jax.numpy as jnp
from jax import lax
from jax.experimental import pallas as pl
from jax.experimental.pallas import tpu as pltpu
from jax.sharding import PartitionSpec as P

LPI = 64
CTF_GAIN = 30.0
PHASE_ZERO = 0.1
STEP_SCALE = 0.5
CHUNK = 128
MESH = pl.DeviceIdType.MESH
F32 = jnp.float32
BF16 = jnp.bfloat16


def sine(x):
    turns = jnp.floor(x * (1.0 / math.pi) + 0.5)
    y = ((x - turns * 3.140625) - turns * 9.67502593994140625e-4) - turns * 1.509957990978376432e-7
    odd = turns - 2.0 * jnp.floor(turns * 0.5)
    y2 = y * y
    poly = -1.0 / 39916800.0
    for inverse in (1.0 / 362880.0, -1.0 / 5040.0, 1.0 / 120.0, -1.0 / 6.0, 1.0):
        poly = poly * y2 + inverse
    return (y * poly) * (1.0 - 2.0 * odd)


def mul_nt(a, b, precision=None):
    return lax.dot_general(
        a, b, (((1,), (1,)), ((), ())), preferred_element_type=F32, precision=precision
    )


def eye(n, kind):
    row = lax.broadcasted_iota(jnp.int32, (n, n), 0)
    col = lax.broadcasted_iota(jnp.int32, (n, n), 1)
    return jnp.where(row == col, 1.0, 0.0).astype(kind)


def remote(src, dst, send, recv, where):
    return pltpu.make_async_remote_copy(
        src_ref=src, dst_ref=dst, send_sem=send, recv_sem=recv, device_id=where, device_id_type=MESH
    )


def build_matrix(taps_ref, wide_ref):
    packed = taps_ref[...].astype(F32)
    value = jnp.concatenate([packed[:8], packed[:8]], axis=0)
    block = jnp.concatenate([packed[8:], packed[8:] - 1.0], axis=0)

    @pl.loop(0, wide_ref.shape[0] // 32)
    def _(t):
        for u in range(2):
            b = (4 * t + 2 * u).astype(F32)
            rows = pl.ds(pl.multiple_of(t * 32 + 16 * u, 16), 16)
            wide_ref[rows, :] = jnp.where(block == b, value, 0.0).astype(BF16)


def kernel(
    n_dom, n_slab, step,
    vol, img, taps, wts, cls, shf, dfc,
    out,
    mapt, omap, ptap, otap, wide, owide, work, proj, square, back,
    gown, s1send, s1recv, s2send, s2recv, gall, cand, ocand, fs, fx, fy, fz,
    tap_s, tap_r, x_s, x_r, y_s, y_r, p_s, p_r, q_s, q_r, g_s, g_r, f_s, f_r, c_s, c_r,
    ux_s, ux_r, uy_s, uy_r, uz_s, uz_r,
):
    h, d, s = lax.axis_index("half"), lax.axis_index("dom"), lax.axis_index("slab")
    lines, cols = vol.shape
    radii = cols // 2
    rows = img.shape[0]
    nz = n_dom // 2
    y, z = lax.rem(d, 2), d // 2
    pair = (h, d + 1 - 2 * y, s)
    other_half = (1 - h, d, s)
    peers = [(h, d, lax.rem(s + p, n_slab)) for p in range(1, n_slab)]
    zs = [lax.rem(z + 1 + t, nz) for t in range(nz)]
    zpeers = [(h, 2 * zs[t] + y, s) for t in range(nz - 1)]
    bw = lines // n_dom
    nj = lines // CHUNK // 2

    barrier = pltpu.get_barrier_semaphore()
    everyone = [pair, other_half] + peers + zpeers
    for who in everyone:
        pl.semaphore_signal(barrier, inc=1, device_id=who, device_id_type=MESH)

    sub = lax.broadcasted_iota(jnp.int32, (8, rows), 0)
    value = jnp.zeros((8, rows), F32)
    block = jnp.zeros((8, rows), F32)
    for k in range(8):
        line = taps[k:k + 1, :]
        hit = jnp.bitwise_and(line, 7) == sub
        value = jnp.where(hit, wts[k:k + 1, :], value)
        block = jnp.where(hit, lax.shift_right_logical(line, 3).astype(F32), block)
    ptap[...] = jnp.concatenate([value, block], axis=0).astype(BF16)

    ident = eye(cols, BF16)

    def map_chunk(c):
        part = vol[pl.ds(pl.multiple_of(c * CHUNK, CHUNK), CHUNK), :].astype(BF16)
        mapt[c] = mul_nt(ident, part).astype(BF16)

    pl.loop(0, 2 * nj)(map_chunk)

    pl.semaphore_wait(barrier, len(everyone))
    sends = []

    def go(copy):
        copy.start()
        sends.append(copy)
        return copy

    tap_copies = [go(remote(ptap, otap.at[p], tap_s.at[p], tap_r.at[p], peers[p])) for p in range(n_slab - 1)]
    x_copies = [
        [
            go(remote(mapt.at[2 * j + y], omap.at[p, 2 * j + y], x_s.at[p, j], x_r.at[p, j], peers[p]))
            for j in range(nj)
        ]
        for p in range(n_slab - 1)
    ]
    y_copies = [[None] * nj for p in range(n_slab - 1)]

    def forward(j):
        for p in range(n_slab - 1):
            x_copies[p][j].wait_recv()
            slot = omap.at[p, 2 * j + y]
            y_copies[p][j] = go(remote(slot, slot, y_s.at[p, j], y_r.at[p, j], pair))

    build_matrix(ptap, wide)

    @pl.loop(0, rows // 256)
    def _(n):
        tile = pl.ds(pl.multiple_of(n * 256, 256), 256)
        work[:, tile] = mul_nt(ident, img[tile, :])
        maps = jnp.concatenate([mapt[c] for c in range(2 * nj)], axis=1)
        proj[:, tile] = jnp.dot(maps, wide[:, tile], preferred_element_type=F32)

    forward(0)

    lane = lax.broadcasted_iota(jnp.int32, (1, rows), 1)
    who = lane // LPI
    focus = jnp.zeros((1, rows), F32)
    shift_x = jnp.zeros((1, rows), F32)
    shift_y = jnp.zeros((1, rows), F32)
    for p in range(rows // LPI):
        mine = who == p
        focus = jnp.where(mine, dfc[cls[0, p]], focus)
        shift_x = jnp.where(mine, shf[0, 0, p].astype(F32), shift_x)
        shift_y = jnp.where(mine, shf[0, 1, p].astype(F32), shift_y)
    theta = (lane - who * LPI).astype(F32) * (math.pi / LPI)
    along = shift_x * sine(theta + 0.5 * math.pi) + shift_y * sine(theta)
    turn = along * (math.pi / radii)
    subf = sub.astype(F32)
    first = subf * turn
    start_re, start_im = sine(first + 0.5 * math.pi), sine(first)
    eighth = 8.0 * turn
    turn_re, turn_im = sine(eighth + 0.5 * math.pi), sine(eighth)

    def phase_step(q, carry):
        e_re, e_im = carry
        re_rows = pl.ds(pl.multiple_of(8 * q, 8), 8)
        im_rows = pl.ds(pl.multiple_of(radii + 8 * q, 8), 8)
        ratio = (subf + (8 * q).astype(F32)) / radii
        ctf = -sine(CTF_GAIN * focus * (ratio * ratio) + PHASE_ZERO)
        im_re, im_im = work[re_rows, :], work[im_rows, :]
        work[re_rows, :] = ctf * (e_re * im_re + e_im * im_im)
        work[im_rows, :] = ctf * (e_re * im_im - e_im * im_re)
        c2 = ctf * ctf
        square[re_rows, :] = c2
        square[im_rows, :] = c2
        return e_re * turn_re - e_im * turn_im, e_re * turn_im + e_im * turn_re

    half_q = radii // 16
    carry = lax.fori_loop(0, half_q, phase_step, (start_re, start_im))
    forward(1)
    lax.fori_loop(half_q, radii // 8, phase_step, carry)

    for p in range(n_slab - 1):
        tap_copies[p].wait_recv()
        build_matrix(otap.at[p], owide)
        for j in range(nj):
            if p == 0 and j + 2 < nj:
                forward(j + 2)
            y_copies[p][j].wait_recv()
            deep = pl.ds(j * 2 * CHUNK, 2 * CHUNK)
            pairs = jnp.concatenate([omap[p, 2 * j], omap[p, 2 * j + 1]], axis=1)

            @pl.loop(0, rows // 256)
            def _(n):
                tile = pl.ds(pl.multiple_of(n * 256, 256), 256)
                proj[:, tile] += jnp.dot(pairs, owide[deep, tile], preferred_element_type=F32)

    @pl.loop(0, cols // 16)
    def _(q):
        at = pl.ds(pl.multiple_of(16 * q, 16), 16)
        back[at, :] = (square[at, :] * proj[at, :] - work[at, :]).astype(BF16)

    def grad_block(b):
        return mul_nt(back[...], wide[pl.ds(pl.multiple_of(b * bw, bw), bw), :])

    p_copies = []
    for t in range(nz):
        s1send[t] = grad_block(2 * zs[t] + 1 - y).astype(BF16)
        p_copies.append(go(remote(s1send.at[t], s1recv.at[t], p_s.at[t], p_r.at[t], pair)))
    q_copies = []
    for t in range(nz):
        gown[t] = grad_block(2 * zs[t] + y)
    for t in range(nz - 1):
        p_copies[t].wait_recv()
        s2send[t] = (gown[t] + s1recv[t].astype(F32)).astype(BF16)
        q_copies.append(go(remote(s2send.at[t], s2recv.at[t], q_s.at[t], q_r.at[t], zpeers[t])))
    p_copies[nz - 1].wait_recv()
    total = gown[nz - 1] + s1recv[nz - 1].astype(F32)
    for t in range(nz - 1):
        q_copies[t].wait_recv()
        total = total + s2recv[t].astype(F32)
    gall[d] = total.astype(BF16)

    g_copies = [go(remote(gall.at[d], gall.at[d], g_s.at[t], g_r.at[t], zpeers[t])) for t in range(nz - 1)]
    f_copies = [go(remote(gall.at[d], gall.at[d], f_s.at[0], f_r.at[0], pair))]

    mine = vol[pl.ds(pl.multiple_of(d * bw, bw), bw), :]
    high = mine.astype(BF16)
    low = (mine - high.astype(F32)).astype(BF16)
    cand_wide = (mul_nt(ident, high) + mul_nt(ident, low)) - step * total
    cand[...] = cand_wide.astype(BF16)
    c_copy = go(remote(cand, ocand, c_s.at[0], c_r.at[0], other_half))
    c_copy.wait_recv()
    theirs = ocand[...].astype(F32)

    def shell(a, b):
        prod = a * b
        prod = prod[:radii] + prod[radii:]
        prod = jnp.concatenate([prod, prod], axis=0)
        return mul_nt(jnp.ones((8, bw), F32), prod, lax.Precision.HIGHEST)

    fs[0] = jnp.concatenate(
        [shell(cand_wide, theirs), shell(cand_wide, cand_wide), shell(theirs, theirs)], axis=0
    )
    ux = [go(remote(fs.at[0], fx.at[p], ux_s.at[p], ux_r.at[p], peers[p])) for p in range(n_slab - 1)]

    def forward_grad(t):
        g_copies[t].wait_recv()
        source = 2 * lax.rem(z + nz - 1 - t, nz) + y
        f_copies.append(go(remote(gall.at[source], gall.at[source], f_s.at[t + 1], f_r.at[t + 1], pair)))

    forward_grad(0)
    sums = fs[0]
    for p in range(n_slab - 1):
        ux[p].wait_recv()
        sums = sums + fx[p]
    fs[1] = sums
    uy = go(remote(fs.at[1], fy, uy_s.at[0], uy_r.at[0], pair))
    if nz > 2:
        forward_grad(1)
    uy.wait_recv()
    sums = sums + fy[...]
    fs[2] = sums
    uz = [go(remote(fs.at[2], fz.at[t], uz_s.at[t], uz_r.at[t], zpeers[t])) for t in range(nz - 1)]
    for t in range(2, nz - 1):
        forward_grad(t)
    for t in range(nz - 1):
        uz[t].wait_recv()
        sums = sums + fz[t]
    num, den_mine, den_other = sums[0:1], sums[8:9], sums[16:17]
    fsc = num / (jnp.sqrt(den_mine * den_other) + 1e-06)
    factor = step * (1.0 + fsc) / 2.0

    for t in range(nz):
        f_copies[t].wait_recv()
    small = eye(bw, BF16)

    @pl.loop(0, n_dom)
    def _(b):
        at = pl.ds(pl.multiple_of(b * bw, bw), bw)
        out[at, :] = vol[at, :] - factor * mul_nt(small, gall[b])

    for copy in sends:
        copy.wait_send()


def body(n_dom, n_slab, volume, images, tap_index, tap_weight, classes, shifts, defocus):
    slab_map, data = volume[0], images[0]
    lines, cols = slab_map.shape
    rows = data.shape[0]
    depth = tap_index.shape[2]
    step = STEP_SCALE / math.sqrt(rows * n_dom * depth / lines)
    nz, bw = n_dom // 2, lines // n_dom
    nc, np_, nj = lines // CHUNK, n_slab - 1, lines // CHUNK // 2
    dma = pltpu.SemaphoreType.DMA
    vmem = pl.BlockSpec(memory_space=pltpu.VMEM)
    smem = pl.BlockSpec(memory_space=pltpu.SMEM)
    scratch = [
        pltpu.VMEM((nc, cols, CHUNK), BF16),
        pltpu.VMEM((np_, nc, cols, CHUNK), BF16),
        pltpu.VMEM((16, rows), BF16),
        pltpu.VMEM((np_, 16, rows), BF16),
        pltpu.VMEM((lines, rows), BF16),
        pltpu.VMEM((lines, rows), BF16),
        pltpu.VMEM((cols, rows), F32),
        pltpu.VMEM((cols, rows), F32),
        pltpu.VMEM((cols, rows), F32),
        pltpu.VMEM((cols, rows), BF16),
        pltpu.VMEM((nz, cols, bw), F32),
        pltpu.VMEM((nz, cols, bw), BF16),
        pltpu.VMEM((nz, cols, bw), BF16),
        pltpu.VMEM((nz - 1, cols, bw), BF16),
        pltpu.VMEM((nz - 1, cols, bw), BF16),
        pltpu.VMEM((n_dom, cols, bw), BF16),
        pltpu.VMEM((cols, bw), BF16),
        pltpu.VMEM((cols, bw), BF16),
        pltpu.VMEM((3, 24, cols), F32),
        pltpu.VMEM((np_, 24, cols), F32),
        pltpu.VMEM((24, cols), F32),
        pltpu.VMEM((nz - 1, 24, cols), F32),
    ]
    for shape in (
        (np_,), (np_, nj), (np_, nj), (nz,), (nz - 1,), (nz - 1,), (nz,), (1,), (np_,), (1,), (nz - 1,)
    ):
        scratch += [dma(shape), dma(shape)]
    result = pl.pallas_call(
        functools.partial(kernel, n_dom, n_slab, step),
        out_shape=jax.ShapeDtypeStruct((lines, cols), F32),
        in_specs=[vmem] * 4 + [smem] * 3,
        out_specs=vmem,
        scratch_shapes=scratch,
        compiler_params=pltpu.CompilerParams(
            collective_id=0, has_side_effects=True, vmem_limit_bytes=56 * 1024 * 1024
        ),
    )(slab_map, data, tap_index[0, 0], tap_weight[0, 0], classes, shifts, defocus)
    return result[None]


def solution(mesh):
    placed = (
        P("half", "slab", None),
        P("half", "dom", None),
        P("half", "slab", None, "dom"),
        P("half", "slab", None, "dom"),
        P("half", "dom"),
        P("half", None, "dom"),
        P(),
    )
    return jax.shard_map(
        functools.partial(body, mesh.shape["dom"], mesh.shape["slab"]),
        mesh=mesh, in_specs=placed, out_specs=P("half", "slab", None), check_vma=False,
    )
```

```python
import functools
import math

import jax
import jax.numpy as jnp
from jax import lax
from jax.experimental import pallas as pl
from jax.experimental.pallas import tpu as pltpu
from jax.sharding import PartitionSpec as P

LPI = 64
CTF_GAIN = 30.0
PHASE_ZERO = 0.1
STEP_SCALE = 0.5
CHUNK = 128
MESH = pl.DeviceIdType.MESH
F32 = jnp.float32
BF16 = jnp.bfloat16


def sine(x):
    turns = jnp.floor(x * (1.0 / math.pi) + 0.5)
    y = ((x - turns * 3.140625) - turns * 9.67502593994140625e-4) - turns * 1.509957990978376432e-7
    odd = turns - 2.0 * jnp.floor(turns * 0.5)
    y2 = y * y
    poly = -1.0 / 39916800.0
    for inverse in (1.0 / 362880.0, -1.0 / 5040.0, 1.0 / 120.0, -1.0 / 6.0, 1.0):
        poly = poly * y2 + inverse
    return (y * poly) * (1.0 - 2.0 * odd)


def mul_nt(a, b, precision=None):
    return lax.dot_general(
        a, b, (((1,), (1,)), ((), ())), preferred_element_type=F32, precision=precision
    )


def eye(n, kind):
    row = lax.broadcasted_iota(jnp.int32, (n, n), 0)
    col = lax.broadcasted_iota(jnp.int32, (n, n), 1)
    return jnp.where(row == col, 1.0, 0.0).astype(kind)


def placing(n, offset):
    row = lax.broadcasted_iota(jnp.int32, (n, CHUNK), 0)
    col = lax.broadcasted_iota(jnp.int32, (n, CHUNK), 1)
    return jnp.where(row + offset == col, 1.0, 0.0).astype(BF16)


def remote(src, dst, send, recv, where):
    return pltpu.make_async_remote_copy(
        src_ref=src, dst_ref=dst, send_sem=send, recv_sem=recv, device_id=where, device_id_type=MESH
    )


def build_matrix(taps_ref, wide_ref):
    packed = taps_ref[...].astype(F32)
    value = jnp.concatenate([packed[:8], packed[:8]], axis=0)
    block = jnp.concatenate([packed[8:], packed[8:] - 1.0], axis=0)

    @pl.loop(0, wide_ref.shape[0] // 32)
    def _(t):
        for u in range(2):
            b = (4 * t + 2 * u).astype(F32)
            rows = pl.ds(pl.multiple_of(t * 32 + 16 * u, 16), 16)
            wide_ref[rows, :] = jnp.where(block == b, value, 0.0).astype(BF16)


def kernel(
    n_dom, n_slab, step,
    vol, img, taps, wts, cls, shf, dfc,
    out,
    mapt, omap, ptap, otap, wide, owide, work, proj, square, back,
    gown, s1send, s1recv, s2send, s2recv, gall, cand, ocand, fs, fx, fy, fz,
    tap_s, tap_r, x_s, x_r, y_s, y_r, z_s, z_r, p_s, p_r, q_s, q_r, g_s, g_r, f_s, f_r, c_s, c_r,
    ux_s, ux_r, uy_s, uy_r, uz_s, uz_r,
):
    h, d, s = lax.axis_index("half"), lax.axis_index("dom"), lax.axis_index("slab")
    cols, lines = vol.shape
    radii = cols // 2
    rows = img.shape[1]
    nz = n_dom // 2
    y, z = lax.rem(d, 2), d // 2
    pair = (h, d + 1 - 2 * y, s)
    other_half = (1 - h, d, s)
    peers = [(h, d, lax.rem(s + p, n_slab)) for p in range(1, n_slab)]
    zs = [lax.rem(z + 1 + t, nz) for t in range(nz)]
    zpeers = [(h, 2 * zs[t] + y, s) for t in range(nz - 1)]
    bw = lines // n_dom
    quarter = lines // CHUNK // 4
    zpair = (h, d + 2 - 4 * lax.rem(z, 2), s)
    mine_q = 2 * lax.rem(z, 2) + y
    y_q, z_q, diag_q = mine_q + 1 - 2 * y, mine_q + 2 - 4 * lax.rem(z, 2), 3 - mine_q

    barrier = pltpu.get_barrier_semaphore()
    everyone = [pair, other_half] + peers + zpeers
    for who in everyone:
        pl.semaphore_signal(barrier, inc=1, device_id=who, device_id_type=MESH)

    sub = lax.broadcasted_iota(jnp.int32, (8, rows), 0)
    value = jnp.zeros((8, rows), F32)
    block = jnp.zeros((8, rows), F32)
    for k in range(8):
        line = taps[k:k + 1, :]
        hit = jnp.bitwise_and(line, 7) == sub
        value = jnp.where(hit, wts[k:k + 1, :], value)
        block = jnp.where(hit, lax.shift_right_logical(line, 3).astype(F32), block)
    ptap[...] = jnp.concatenate([value, block], axis=0).astype(BF16)

    @pl.loop(0, lines // CHUNK)
    def _(c):
        mapt[c] = vol[:, pl.ds(pl.multiple_of(c * CHUNK, CHUNK), CHUNK)].astype(BF16)

    pl.semaphore_wait(barrier, len(everyone))
    sends = []

    def go(copy):
        copy.start()
        sends.append(copy)
        return copy

    tap_copies = [go(remote(ptap, otap.at[p], tap_s.at[p], tap_r.at[p], peers[p])) for p in range(n_slab - 1)]
    x_copies = [
        [
            go(remote(mapt.at[c], omap.at[p, c], x_s.at[p, i], x_r.at[p, i], peers[p]))
            for i, c in enumerate([g * quarter + u for g in (mine_q, diag_q) for u in range(quarter)])
        ]
        for p in range(n_slab - 1)
    ]
    y_copies = [[None] * quarter for p in range(n_slab - 1)]
    z_copies = [[None] * quarter for p in range(n_slab - 1)]

    def forward(u):
        for p in range(n_slab - 1):
            x_copies[p][u].wait_recv()
            slot = omap.at[p, mine_q * quarter + u]
            y_copies[p][u] = go(remote(slot, slot, y_s.at[p, u], y_r.at[p, u], pair))
            z_copies[p][u] = go(remote(slot, slot, z_s.at[p, u], z_r.at[p, u], zpair))

    build_matrix(ptap, wide)

    @pl.loop(0, rows // 256)
    def _(n):
        tile = pl.ds(pl.multiple_of(n * 256, 256), 256)
        work[:, tile] = img[:, tile].astype(F32)
        maps = jnp.concatenate([mapt[c] for c in range(4 * quarter)], axis=1)
        proj[:, tile] = jnp.dot(maps, wide[:, tile], preferred_element_type=F32)

    forward(0)

    lane = lax.broadcasted_iota(jnp.int32, (1, rows), 1)
    who = lane // LPI
    focus = jnp.zeros((1, rows), F32)
    shift_x = jnp.zeros((1, rows), F32)
    shift_y = jnp.zeros((1, rows), F32)
    for p in range(rows // LPI):
        mine = who == p
        focus = jnp.where(mine, dfc[cls[0, p]], focus)
        shift_x = jnp.where(mine, shf[0, 0, p].astype(F32), shift_x)
        shift_y = jnp.where(mine, shf[0, 1, p].astype(F32), shift_y)
    theta = (lane - who * LPI).astype(F32) * (math.pi / LPI)
    along = shift_x * sine(theta + 0.5 * math.pi) + shift_y * sine(theta)
    turn = along * (math.pi / radii)
    subf = sub.astype(F32)
    first = subf * turn
    start_re, start_im = sine(first + 0.5 * math.pi), sine(first)
    eighth = 8.0 * turn
    turn_re, turn_im = sine(eighth + 0.5 * math.pi), sine(eighth)

    def phase_step(q, carry):
        e_re, e_im = carry
        re_rows = pl.ds(pl.multiple_of(8 * q, 8), 8)
        im_rows = pl.ds(pl.multiple_of(radii + 8 * q, 8), 8)
        ratio = (subf + (8 * q).astype(F32)) / radii
        ctf = -sine(CTF_GAIN * focus * (ratio * ratio) + PHASE_ZERO)
        im_re, im_im = work[re_rows, :], work[im_rows, :]
        work[re_rows, :] = ctf * (e_re * im_re + e_im * im_im)
        work[im_rows, :] = ctf * (e_re * im_im - e_im * im_re)
        c2 = ctf * ctf
        square[re_rows, :] = c2
        square[im_rows, :] = c2
        return e_re * turn_re - e_im * turn_im, e_re * turn_im + e_im * turn_re

    half_q = radii // 16
    carry = lax.fori_loop(0, half_q, phase_step, (start_re, start_im))
    for u in range(1, quarter):
        forward(u)
    lax.fori_loop(half_q, radii // 8, phase_step, carry)

    for p in range(n_slab - 1):
        tap_copies[p].wait_recv()
        build_matrix(otap.at[p], owide)
        for g, copies in (
            (mine_q, []), (y_q, y_copies[p]), (z_q, z_copies[p]), (diag_q, x_copies[p][quarter:])
        ):
            for copy in copies:
                copy.wait_recv()
            depth = quarter * CHUNK
            deep = pl.ds(pl.multiple_of(g * depth, depth), depth)
            maps = jnp.concatenate([omap[p, g * quarter + u] for u in range(quarter)], axis=1)

            @pl.loop(0, rows // 256)
            def _(n):
                tile = pl.ds(pl.multiple_of(n * 256, 256), 256)
                proj[:, tile] += jnp.dot(maps, owide[deep, tile], preferred_element_type=F32)

    @pl.loop(0, cols // 16)
    def _(q):
        at = pl.ds(pl.multiple_of(16 * q, 16), 16)
        back[at, :] = (square[at, :] * proj[at, :] - work[at, :]).astype(BF16)

    def grad_block(b):
        return mul_nt(back[...], wide[pl.ds(pl.multiple_of(b * bw, bw), bw), :])

    p_copies = []
    for t in range(nz):
        s1send[t] = grad_block(2 * zs[t] + 1 - y).astype(BF16)
        p_copies.append(go(remote(s1send.at[t], s1recv.at[t], p_s.at[t], p_r.at[t], pair)))
    q_copies = []
    for t in range(nz):
        gown[t] = grad_block(2 * zs[t] + y)
    for t in range(nz - 1):
        p_copies[t].wait_recv()
        s2send[t] = (gown[t] + s1recv[t].astype(F32)).astype(BF16)
        q_copies.append(go(remote(s2send.at[t], s2recv.at[t], q_s.at[t], q_r.at[t], zpeers[t])))
    p_copies[nz - 1].wait_recv()
    total = gown[nz - 1] + s1recv[nz - 1].astype(F32)
    for t in range(nz - 1):
        q_copies[t].wait_recv()
        total = total + s2recv[t].astype(F32)
    gall[d] = total.astype(BF16)

    g_copies = [go(remote(gall.at[d], gall.at[d], g_s.at[t], g_r.at[t], zpeers[t])) for t in range(nz - 1)]
    f_copies = [go(remote(gall.at[d], gall.at[d], f_s.at[0], f_r.at[0], pair))]

    if bw % CHUNK == 0:
        mine = vol[:, pl.ds(pl.multiple_of(d * bw, CHUNK), bw)]
    else:
        at = (d * bw) // CHUNK
        near = vol[:, pl.ds(pl.multiple_of(at * CHUNK, CHUNK), CHUNK)]
        high = near.astype(BF16)
        low = (near - high.astype(F32)).astype(BF16)
        pick = placing(bw, d * bw - at * CHUNK)
        mine = mul_nt(high, pick) + mul_nt(low, pick)
    cand_wide = mine - step * total
    cand[...] = cand_wide.astype(BF16)
    c_copy = go(remote(cand, ocand, c_s.at[0], c_r.at[0], other_half))
    c_copy.wait_recv()
    theirs = ocand[...].astype(F32)

    def shell(a, b):
        prod = a * b
        prod = prod[:radii] + prod[radii:]
        return mul_nt(jnp.ones((8, bw), F32), prod, lax.Precision.HIGHEST)

    kind = lax.broadcasted_iota(jnp.int32, (8, radii), 0)
    den_mine, den_other = shell(cand_wide, cand_wide), shell(theirs, theirs)
    fs[0] = jnp.where(kind == 0, shell(cand_wide, theirs), jnp.where(kind == 1, den_mine, den_other))
    ux = [go(remote(fs.at[0], fx.at[p], ux_s.at[p], ux_r.at[p], peers[p])) for p in range(n_slab - 1)]

    def forward_grad(t):
        g_copies[t].wait_recv()
        source = 2 * lax.rem(z + nz - 1 - t, nz) + y
        f_copies.append(go(remote(gall.at[source], gall.at[source], f_s.at[t + 1], f_r.at[t + 1], pair)))

    forward_grad(0)
    sums = fs[0]
    for p in range(n_slab - 1):
        ux[p].wait_recv()
        sums = sums + fx[p]
    fs[1] = sums
    uy = go(remote(fs.at[1], fy, uy_s.at[0], uy_r.at[0], pair))
    if nz > 2:
        forward_grad(1)
    uy.wait_recv()
    sums = sums + fy[...]
    fs[2] = sums
    uz = [go(remote(fs.at[2], fz.at[t], uz_s.at[t], uz_r.at[t], zpeers[t])) for t in range(nz - 1)]
    for t in range(2, nz - 1):
        forward_grad(t)
    for t in range(nz - 1):
        uz[t].wait_recv()
        sums = sums + fz[t]
    num, den_mine, den_other = sums[0:1], sums[1:2], sums[2:3]
    fsc = num / (jnp.sqrt(den_mine * den_other) + 1e-06)
    factor = step * (1.0 + fsc) / 2.0
    column = jnp.sum(eye(radii, F32) * factor, axis=1, keepdims=True)
    column = jnp.concatenate([column, column], axis=0)

    for t in range(nz):
        f_copies[t].wait_recv()
    if bw % CHUNK == 0:
        @pl.loop(0, n_dom)
        def _(b):
            at = pl.ds(pl.multiple_of(b * bw, CHUNK), bw)
            out[:, at] = vol[:, at] - column * gall[b].astype(F32)
    else:
        share = CHUNK // bw

        @pl.loop(0, lines // CHUNK)
        def _(c):
            at = pl.ds(pl.multiple_of(c * CHUNK, CHUNK), CHUNK)
            whole = jnp.zeros((cols, CHUNK), F32)
            for u in range(share):
                whole = whole + jnp.dot(gall[c * share + u], placing(bw, u * bw), preferred_element_type=F32)
            out[:, at] = vol[:, at] - column * whole

    for copy in sends:
        copy.wait_send()


def body(n_dom, n_slab, volume, images, tap_index, tap_weight, classes, shifts, defocus):
    slab_map, data = volume[0].T, images[0].T
    cols, lines = slab_map.shape
    rows = data.shape[1]
    depth = tap_index.shape[2]
    step = STEP_SCALE / math.sqrt(rows * n_dom * depth / lines)
    nz, bw = n_dom // 2, lines // n_dom
    nc, np_, nq = lines // CHUNK, n_slab - 1, lines // CHUNK // 4
    dma = pltpu.SemaphoreType.DMA
    vmem = pl.BlockSpec(memory_space=pltpu.VMEM)
    smem = pl.BlockSpec(memory_space=pltpu.SMEM)
    scratch = [
        pltpu.VMEM((nc, cols, CHUNK), BF16),
        pltpu.VMEM((np_, nc, cols, CHUNK), BF16),
        pltpu.VMEM((16, rows), BF16),
        pltpu.VMEM((np_, 16, rows), BF16),
        pltpu.VMEM((lines, rows), BF16),
        pltpu.VMEM((lines, rows), BF16),
        pltpu.VMEM((cols, rows), F32),
        pltpu.VMEM((cols, rows), F32),
        pltpu.VMEM((cols, rows), F32),
        pltpu.VMEM((cols, rows), BF16),
        pltpu.VMEM((nz, cols, bw), F32),
        pltpu.VMEM((nz, cols, bw), BF16),
        pltpu.VMEM((nz, cols, bw), BF16),
        pltpu.VMEM((nz - 1, cols, bw), BF16),
        pltpu.VMEM((nz - 1, cols, bw), BF16),
        pltpu.VMEM((n_dom, cols, bw), BF16),
        pltpu.VMEM((cols, bw), BF16),
        pltpu.VMEM((cols, bw), BF16),
        pltpu.VMEM((3, 8, cols // 2), F32),
        pltpu.VMEM((np_, 8, cols // 2), F32),
        pltpu.VMEM((8, cols // 2), F32),
        pltpu.VMEM((nz - 1, 8, cols // 2), F32),
    ]
    for shape in (
        (np_,), (np_, 2 * nq), (np_, nq), (np_, nq), (nz,), (nz - 1,), (nz - 1,), (nz,), (1,), (np_,), (1,), (nz - 1,)
    ):
        scratch += [dma(shape), dma(shape)]
    result = pl.pallas_call(
        functools.partial(kernel, n_dom, n_slab, step),
        out_shape=jax.ShapeDtypeStruct((cols, lines), F32),
        in_specs=[vmem] * 4 + [smem] * 3,
        out_specs=vmem,
        scratch_shapes=scratch,
        compiler_params=pltpu.CompilerParams(
            collective_id=0, has_side_effects=True, vmem_limit_bytes=56 * 1024 * 1024
        ),
    )(slab_map, data, tap_index[0, 0], tap_weight[0, 0], classes, shifts, defocus)
    return result.T[None]


def solution(mesh):
    placed = (
        P("half", "slab", None),
        P("half", "dom", None),
        P("half", "slab", None, "dom"),
        P("half", "slab", None, "dom"),
        P("half", "dom"),
        P("half", None, "dom"),
        P(),
    )
    return jax.shard_map(
        functools.partial(body, mesh.shape["dom"], mesh.shape["slab"]),
        mesh=mesh, in_specs=placed, out_specs=P("half", "slab", None), check_vma=False,
    )
```

```python
import functools
import math

import jax
import jax.numpy as jnp
from jax import lax
from jax.experimental import pallas as pl
from jax.experimental.pallas import tpu as pltpu
from jax.sharding import PartitionSpec as P

LPI = 64
CTF_GAIN = 30.0
PHASE_ZERO = 0.1
STEP_SCALE = 0.5
CHUNK = 128
MESH = pl.DeviceIdType.MESH
F32 = jnp.float32
BF16 = jnp.bfloat16


def sine(x):
    turns = jnp.floor(x * (1.0 / math.pi) + 0.5)
    y = ((x - turns * 3.140625) - turns * 9.67502593994140625e-4) - turns * 1.509957990978376432e-7
    odd = turns - 2.0 * jnp.floor(turns * 0.5)
    y2 = y * y
    poly = -1.0 / 39916800.0
    for inverse in (1.0 / 362880.0, -1.0 / 5040.0, 1.0 / 120.0, -1.0 / 6.0, 1.0):
        poly = poly * y2 + inverse
    return (y * poly) * (1.0 - 2.0 * odd)


def mul_nt(a, b, precision=None):
    return lax.dot_general(
        a, b, (((1,), (1,)), ((), ())), preferred_element_type=F32, precision=precision
    )


def eye(n, kind):
    row = lax.broadcasted_iota(jnp.int32, (n, n), 0)
    col = lax.broadcasted_iota(jnp.int32, (n, n), 1)
    return jnp.where(row == col, 1.0, 0.0).astype(kind)


def placing(n, offset):
    row = lax.broadcasted_iota(jnp.int32, (n, CHUNK), 0)
    col = lax.broadcasted_iota(jnp.int32, (n, CHUNK), 1)
    return jnp.where(row + offset == col, 1.0, 0.0).astype(BF16)


def remote(src, dst, send, recv, where):
    return pltpu.make_async_remote_copy(
        src_ref=src, dst_ref=dst, send_sem=send, recv_sem=recv, device_id=where, device_id_type=MESH
    )


def build_matrix(taps_ref, wide_ref):
    packed = taps_ref[...].astype(F32)
    value = jnp.concatenate([packed[:8], packed[:8]], axis=0)
    block = jnp.concatenate([packed[8:], packed[8:] - 1.0], axis=0)

    @pl.loop(0, wide_ref.shape[0] // 32)
    def _(t):
        for u in range(2):
            b = (4 * t + 2 * u).astype(F32)
            rows = pl.ds(pl.multiple_of(t * 32 + 16 * u, 16), 16)
            wide_ref[rows, :] = jnp.where(block == b, value, 0.0).astype(BF16)


def kernel(
    n_dom, n_slab, step,
    vol, img, taps, wts, cls, shf, dfc,
    out,
    mapt, omap, ptap, otap, wide, owide, work, proj, square, back,
    gown, s1send, s1recv, s2send, s2recv, gall, cand, ocand, fs, fx, fy, fz,
    tap_s, tap_r, x_s, x_r, y_s, y_r, z_s, z_r, p_s, p_r, q_s, q_r, g_s, g_r, f_s, f_r, c_s, c_r,
    ux_s, ux_r, uy_s, uy_r, uz_s, uz_r,
):
    h, d, s = lax.axis_index("half"), lax.axis_index("dom"), lax.axis_index("slab")
    cols, lines = vol.shape
    radii = cols // 2
    rows = img.shape[1]
    nz = n_dom // 2
    y, z = lax.rem(d, 2), d // 2
    pair = (h, d + 1 - 2 * y, s)
    other_half = (1 - h, d, s)
    peers = [(h, d, lax.rem(s + p, n_slab)) for p in range(1, n_slab)]
    zs = [lax.rem(z + 1 + t, nz) for t in range(nz)]
    zpeers = [(h, 2 * zs[t] + y, s) for t in range(nz - 1)]
    bw = lines // n_dom
    quarter = lines // CHUNK // 4
    zpair = (h, d + 2 - 4 * lax.rem(z, 2), s)
    mine_q = 2 * lax.rem(z, 2) + y
    y_q, z_q, diag_q = mine_q + 1 - 2 * y, mine_q + 2 - 4 * lax.rem(z, 2), 3 - mine_q

    barrier = pltpu.get_barrier_semaphore()
    everyone = [pair, other_half] + peers + zpeers
    for who in everyone:
        pl.semaphore_signal(barrier, inc=1, device_id=who, device_id_type=MESH)

    sub = lax.broadcasted_iota(jnp.int32, (8, rows), 0)
    value = jnp.zeros((8, rows), F32)
    block = jnp.zeros((8, rows), F32)
    for k in range(8):
        line = taps[k:k + 1, :]
        hit = jnp.bitwise_and(line, 7) == sub
        value = jnp.where(hit, wts[k:k + 1, :], value)
        block = jnp.where(hit, lax.shift_right_logical(line, 3).astype(F32), block)
    ptap[...] = jnp.concatenate([value, block], axis=0).astype(BF16)

    @pl.loop(0, lines // CHUNK)
    def _(c):
        mapt[c] = vol[:, pl.ds(pl.multiple_of(c * CHUNK, CHUNK), CHUNK)].astype(BF16)

    pl.semaphore_wait(barrier, len(everyone))
    sends = []

    def go(copy, needed=None):
        if needed is None:
            copy.start()
        else:
            pl.when(needed)(copy.start)
        sends.append((copy, needed))
        return copy

    tap_copies = [go(remote(ptap, otap.at[p], tap_s.at[p], tap_r.at[p], peers[p])) for p in range(n_slab - 1)]
    x_copies = [
        [
            go(remote(mapt.at[c], omap.at[p, c], x_s.at[p, i], x_r.at[p, i], peers[p]))
            for i, c in enumerate([g * quarter + u for g in (mine_q, diag_q) for u in range(quarter)])
        ]
        for p in range(n_slab - 1)
    ]
    y_copies = [[None] * quarter for p in range(n_slab - 1)]
    z_copies = [[None] * quarter for p in range(n_slab - 1)]

    def forward(u):
        for p in range(n_slab - 1):
            x_copies[p][u].wait_recv()
            slot = omap.at[p, mine_q * quarter + u]
            y_copies[p][u] = go(remote(slot, slot, y_s.at[p, u], y_r.at[p, u], pair))
            z_copies[p][u] = go(remote(slot, slot, z_s.at[p, u], z_r.at[p, u], zpair))

    build_matrix(ptap, wide)
    forward(0)

    @pl.loop(0, rows // 256)
    def _(n):
        tile = pl.ds(pl.multiple_of(n * 256, 256), 256)
        work[:, tile] = img[:, tile].astype(F32)
        maps = jnp.concatenate([mapt[c] for c in range(4 * quarter)], axis=1)
        proj[:, tile] = jnp.dot(maps, wide[:, tile], preferred_element_type=F32)

    for u in range(1, quarter):
        forward(u)

    lane = lax.broadcasted_iota(jnp.int32, (1, rows), 1)
    who = lane // LPI
    focus = jnp.zeros((1, rows), F32)
    shift_x = jnp.zeros((1, rows), F32)
    shift_y = jnp.zeros((1, rows), F32)
    for p in range(rows // LPI):
        mine = who == p
        focus = jnp.where(mine, dfc[cls[0, p]], focus)
        shift_x = jnp.where(mine, shf[0, 0, p].astype(F32), shift_x)
        shift_y = jnp.where(mine, shf[0, 1, p].astype(F32), shift_y)
    theta = (lane - who * LPI).astype(F32) * (math.pi / LPI)
    along = shift_x * sine(theta + 0.5 * math.pi) + shift_y * sine(theta)
    turn = along * (math.pi / radii)
    subf = sub.astype(F32)
    first = subf * turn
    start_re, start_im = sine(first + 0.5 * math.pi), sine(first)
    eighth = 8.0 * turn
    turn_re, turn_im = sine(eighth + 0.5 * math.pi), sine(eighth)

    def phase_step(q, carry):
        e_re, e_im = carry
        re_rows = pl.ds(pl.multiple_of(8 * q, 8), 8)
        im_rows = pl.ds(pl.multiple_of(radii + 8 * q, 8), 8)
        ratio = (subf + (8 * q).astype(F32)) / radii
        ctf = -sine(CTF_GAIN * focus * (ratio * ratio) + PHASE_ZERO)
        im_re, im_im = work[re_rows, :], work[im_rows, :]
        work[re_rows, :] = ctf * (e_re * im_re + e_im * im_im)
        work[im_rows, :] = ctf * (e_re * im_im - e_im * im_re)
        c2 = ctf * ctf
        square[re_rows, :] = c2
        square[im_rows, :] = c2
        return e_re * turn_re - e_im * turn_im, e_re * turn_im + e_im * turn_re

    lax.fori_loop(0, radii // 8, phase_step, (start_re, start_im))

    for p in range(n_slab - 1):
        tap_copies[p].wait_recv()
        build_matrix(otap.at[p], owide)
        for g, copies in (
            (mine_q, []), (y_q, y_copies[p]), (z_q, z_copies[p]), (diag_q, x_copies[p][quarter:])
        ):
            for copy in copies:
                copy.wait_recv()
            depth = quarter * CHUNK
            deep = pl.ds(pl.multiple_of(g * depth, depth), depth)
            maps = jnp.concatenate([omap[p, g * quarter + u] for u in range(quarter)], axis=1)

            @pl.loop(0, rows // 256)
            def _(n):
                tile = pl.ds(pl.multiple_of(n * 256, 256), 256)
                proj[:, tile] += jnp.dot(maps, owide[deep, tile], preferred_element_type=F32)

    @pl.loop(0, cols // 16)
    def _(q):
        at = pl.ds(pl.multiple_of(16 * q, 16), 16)
        back[at, :] = (square[at, :] * proj[at, :] - work[at, :]).astype(BF16)

    def grad_block(b):
        return mul_nt(back[...], wide[pl.ds(pl.multiple_of(b * bw, bw), bw), :])

    p_copies = []
    for t in range(nz):
        s1send[t] = grad_block(2 * zs[t] + 1 - y).astype(BF16)
        p_copies.append(go(remote(s1send.at[t], s1recv.at[t], p_s.at[t], p_r.at[t], pair)))
    q_copies = []
    for t in range(nz):
        gown[t] = grad_block(2 * zs[t] + y)
    for t in range(nz - 1):
        p_copies[t].wait_recv()
        s2send[t] = (gown[t] + s1recv[t].astype(F32)).astype(BF16)
        q_copies.append(go(remote(s2send.at[t], s2recv.at[t], q_s.at[t], q_r.at[t], zpeers[t])))
    p_copies[nz - 1].wait_recv()
    total = gown[nz - 1] + s1recv[nz - 1].astype(F32)
    for t in range(nz - 1):
        q_copies[t].wait_recv()
        total = total + s2recv[t].astype(F32)
    gall[d] = total.astype(BF16)

    middle = cols // 32 * 16
    parts = ((0, middle), (middle, cols - middle))
    to_right, to_left = (h, d + 2, s), (h, d - 2, s)

    def share(zz, u):
        return gall.at[2 * zz + y, pl.ds(*parts[u]), :]

    def relay(k, u):
        for way, where, source, needed in (
            (0, to_right, z - k, jnp.logical_and(z - k >= 0, z + 1 < nz)),
            (1, to_left, z + k, jnp.logical_and(z + k < nz, z >= 1)),
        ):
            part = share(source, u)
            go(remote(part, part, g_s.at[way, k, u], g_r.at[way, k, u], where), needed)

    def from_pair(way, k, u, source, needed):
        part = share(source, u)
        pair_copies.append((go(remote(part, part, f_s.at[way, k, u], f_r.at[way, k, u], pair), needed), needed))

    pair_copies = []
    for u in range(2):
        relay(0, u)
        from_pair(0, 0, u, z, None)

    def arrive(k):
        for u in range(2):
            for way, source, needed in ((0, z - k, z - k >= 0), (1, z + k, z + k < nz)):
                part = share(source, u)
                come = remote(part, part, g_s.at[way, k - 1, u], g_r.at[way, k - 1, u], pair)
                pl.when(needed)(come.wait_recv)
                from_pair(way, k, u, source, needed)
            if k < nz - 1:
                relay(k, u)

    if bw % CHUNK == 0:
        mine = vol[:, pl.ds(pl.multiple_of(d * bw, CHUNK), bw)]
    else:
        at = (d * bw) // CHUNK
        near = vol[:, pl.ds(pl.multiple_of(at * CHUNK, CHUNK), CHUNK)]
        high = near.astype(BF16)
        low = (near - high.astype(F32)).astype(BF16)
        pick = placing(bw, d * bw - at * CHUNK)
        mine = mul_nt(high, pick) + mul_nt(low, pick)
    cand_wide = mine - step * total
    cand[...] = cand_wide.astype(BF16)
    c_copy = go(remote(cand, ocand, c_s.at[0], c_r.at[0], other_half))
    c_copy.wait_recv()
    theirs = ocand[...].astype(F32)

    def shell(a, b):
        prod = a * b
        prod = prod[:radii] + prod[radii:]
        return mul_nt(jnp.ones((8, bw), F32), prod, lax.Precision.HIGHEST)

    kind = lax.broadcasted_iota(jnp.int32, (8, radii), 0)
    den_mine, den_other = shell(cand_wide, cand_wide), shell(theirs, theirs)
    fs[0] = jnp.where(kind == 0, shell(cand_wide, theirs), jnp.where(kind == 1, den_mine, den_other))
    ux = [go(remote(fs.at[0], fx.at[p], ux_s.at[p], ux_r.at[p], peers[p])) for p in range(n_slab - 1)]

    arrive(1)
    sums = fs[0]
    for p in range(n_slab - 1):
        ux[p].wait_recv()
        sums = sums + fx[p]
    fs[1] = sums
    uy = go(remote(fs.at[1], fy, uy_s.at[0], uy_r.at[0], pair))
    if nz > 2:
        arrive(2)
    uy.wait_recv()
    sums = sums + fy[...]
    fs[2] = sums
    uz = [go(remote(fs.at[2], fz.at[t], uz_s.at[t], uz_r.at[t], zpeers[t])) for t in range(nz - 1)]
    for k in range(3, nz):
        arrive(k)
    for t in range(nz - 1):
        uz[t].wait_recv()
        sums = sums + fz[t]
    num, den_mine, den_other = sums[0:1], sums[1:2], sums[2:3]
    fsc = num / (jnp.sqrt(den_mine * den_other) + 1e-06)
    factor = step * (1.0 + fsc) / 2.0
    column = jnp.sum(eye(radii, F32) * factor, axis=1, keepdims=True)
    column = jnp.concatenate([column, column], axis=0)

    for copy, needed in pair_copies:
        if needed is None:
            copy.wait_recv()
        else:
            pl.when(needed)(copy.wait_recv)
    if bw % CHUNK == 0:
        for b in range(n_dom):
            out[:, b * bw:(b + 1) * bw] = column * gall[b].astype(F32)
    else:
        fold = CHUNK // bw

        @pl.loop(0, lines // CHUNK)
        def _(c):
            whole = jnp.zeros((cols, CHUNK), F32)
            for u in range(fold):
                whole = whole + jnp.dot(gall[c * fold + u], placing(bw, u * bw), preferred_element_type=F32)
            out[:, pl.ds(pl.multiple_of(c * CHUNK, CHUNK), CHUNK)] = column * whole

    for copy, needed in sends:
        if needed is None:
            copy.wait_send()
        else:
            pl.when(needed)(copy.wait_send)


def body(n_dom, n_slab, volume, images, tap_index, tap_weight, classes, shifts, defocus):
    slab_map, data = volume[0].T, images[0].T
    cols, lines = slab_map.shape
    rows = data.shape[1]
    depth = tap_index.shape[2]
    step = STEP_SCALE / math.sqrt(rows * n_dom * depth / lines)
    nz, bw = n_dom // 2, lines // n_dom
    nc, np_, nq = lines // CHUNK, n_slab - 1, lines // CHUNK // 4
    dma = pltpu.SemaphoreType.DMA
    vmem = pl.BlockSpec(memory_space=pltpu.VMEM)
    smem = pl.BlockSpec(memory_space=pltpu.SMEM)
    scratch = [
        pltpu.VMEM((nc, cols, CHUNK), BF16),
        pltpu.VMEM((np_, nc, cols, CHUNK), BF16),
        pltpu.VMEM((16, rows), BF16),
        pltpu.VMEM((np_, 16, rows), BF16),
        pltpu.VMEM((lines, rows), BF16),
        pltpu.VMEM((lines, rows), BF16),
        pltpu.VMEM((cols, rows), F32),
        pltpu.VMEM((cols, rows), F32),
        pltpu.VMEM((cols, rows), F32),
        pltpu.VMEM((cols, rows), BF16),
        pltpu.VMEM((nz, cols, bw), F32),
        pltpu.VMEM((nz, cols, bw), BF16),
        pltpu.VMEM((nz, cols, bw), BF16),
        pltpu.VMEM((nz - 1, cols, bw), BF16),
        pltpu.VMEM((nz - 1, cols, bw), BF16),
        pltpu.VMEM((n_dom, cols, bw), BF16),
        pltpu.VMEM((cols, bw), BF16),
        pltpu.VMEM((cols, bw), BF16),
        pltpu.VMEM((3, 8, cols // 2), F32),
        pltpu.VMEM((np_, 8, cols // 2), F32),
        pltpu.VMEM((8, cols // 2), F32),
        pltpu.VMEM((nz - 1, 8, cols // 2), F32),
    ]
    for shape in (
        (np_,), (np_, 2 * nq), (np_, nq), (np_, nq), (nz,), (nz - 1,), (2, nz - 1, 2), (2, nz, 2), (1,), (np_,), (1,), (nz - 1,)
    ):
        scratch += [dma(shape), dma(shape)]
    change = pl.pallas_call(
        functools.partial(kernel, n_dom, n_slab, step),
        out_shape=jax.ShapeDtypeStruct((cols, lines), F32),
        in_specs=[vmem] * 4 + [smem] * 3,
        out_specs=vmem,
        scratch_shapes=scratch,
        compiler_params=pltpu.CompilerParams(
            collective_id=0, has_side_effects=True, vmem_limit_bytes=56 * 1024 * 1024
        ),
    )(slab_map, data, tap_index[0, 0], tap_weight[0, 0], classes, shifts, defocus)
    return (slab_map - change).T[None]


def solution(mesh):
    placed = (
        P("half", "slab", None),
        P("half", "dom", None),
        P("half", "slab", None, "dom"),
        P("half", "slab", None, "dom"),
        P("half", "dom"),
        P("half", None, "dom"),
        P(),
    )
    return jax.shard_map(
        functools.partial(body, mesh.shape["dom"], mesh.shape["slab"]),
        mesh=mesh, in_specs=placed, out_specs=P("half", "slab", None), check_vma=False,
    )
```

```python
import functools
import math

import jax
import jax.numpy as jnp
from jax import lax
from jax.experimental import pallas as pl
from jax.experimental.pallas import tpu as pltpu
from jax.sharding import PartitionSpec as P

LPI = 64
CTF_GAIN = 30.0
PHASE_ZERO = 0.1
STEP_SCALE = 0.5
CHUNK = 128
MESH = pl.DeviceIdType.MESH
F32 = jnp.float32
BF16 = jnp.bfloat16


def sine(x):
    turns = jnp.floor(x * (1.0 / math.pi) + 0.5)
    y = ((x - turns * 3.140625) - turns * 9.67502593994140625e-4) - turns * 1.509957990978376432e-7
    odd = turns - 2.0 * jnp.floor(turns * 0.5)
    y2 = y * y
    poly = -1.0 / 39916800.0
    for inverse in (1.0 / 362880.0, -1.0 / 5040.0, 1.0 / 120.0, -1.0 / 6.0, 1.0):
        poly = poly * y2 + inverse
    return (y * poly) * (1.0 - 2.0 * odd)


def mul_nt(a, b, precision=None):
    return lax.dot_general(
        a, b, (((1,), (1,)), ((), ())), preferred_element_type=F32, precision=precision
    )


def eye(n, kind):
    row = lax.broadcasted_iota(jnp.int32, (n, n), 0)
    col = lax.broadcasted_iota(jnp.int32, (n, n), 1)
    return jnp.where(row == col, 1.0, 0.0).astype(kind)


def placing(n, offset):
    row = lax.broadcasted_iota(jnp.int32, (n, CHUNK), 0)
    col = lax.broadcasted_iota(jnp.int32, (n, CHUNK), 1)
    return jnp.where(row + offset == col, 1.0, 0.0).astype(BF16)


def remote(src, dst, send, recv, where):
    return pltpu.make_async_remote_copy(
        src_ref=src, dst_ref=dst, send_sem=send, recv_sem=recv, device_id=where, device_id_type=MESH
    )


def build_matrix(taps_ref, wide_ref):
    packed = taps_ref[...].astype(F32)
    value = jnp.concatenate([packed[:8], packed[:8]], axis=0)
    block = jnp.concatenate([packed[8:], packed[8:] - 1.0], axis=0)

    @pl.loop(0, wide_ref.shape[0] // 32)
    def _(t):
        for u in range(2):
            b = (4 * t + 2 * u).astype(F32)
            rows = pl.ds(pl.multiple_of(t * 32 + 16 * u, 16), 16)
            wide_ref[rows, :] = jnp.where(block == b, value, 0.0).astype(BF16)


def kernel(
    n_dom, n_slab, step,
    vol, img, taps, wts, cls, shf, dfc,
    out,
    mapt, omap, ptap, otap, wide, owide, work, proj, square, back,
    gown, s1send, s1recv, s2send, s2recv, gall, cand, ocand, fs, fx, fy, fz,
    tap_s, tap_r, x_s, x_r, y_s, y_r, z_s, z_r, p_s, p_r, q_s, q_r, g_s, g_r, f_s, f_r, c_s, c_r,
    ux_s, ux_r, uy_s, uy_r, uz_s, uz_r,
):
    h, d, s = lax.axis_index("half"), lax.axis_index("dom"), lax.axis_index("slab")
    cols, lines = vol.shape
    radii = cols // 2
    rows = img.shape[1]
    nz = n_dom // 2
    y, z = lax.rem(d, 2), d // 2
    pair = (h, d + 1 - 2 * y, s)
    other_half = (1 - h, d, s)
    peers = [(h, d, lax.rem(s + p, n_slab)) for p in range(1, n_slab)]
    zs = [lax.rem(z + 1 + t, nz) for t in range(nz)]
    zpeers = [(h, 2 * zs[t] + y, s) for t in range(nz - 1)]
    bw = lines // n_dom
    quarter = lines // CHUNK // 4
    zpair = (h, d + 2 - 4 * lax.rem(z, 2), s)
    mine_q = 2 * lax.rem(z, 2) + y
    y_q, z_q, diag_q = mine_q + 1 - 2 * y, mine_q + 2 - 4 * lax.rem(z, 2), 3 - mine_q

    barrier = pltpu.get_barrier_semaphore()
    everyone = [pair, other_half] + peers + zpeers
    for who in everyone:
        pl.semaphore_signal(barrier, inc=1, device_id=who, device_id_type=MESH)

    sub = lax.broadcasted_iota(jnp.int32, (8, rows), 0)
    value = jnp.zeros((8, rows), F32)
    block = jnp.zeros((8, rows), F32)
    for k in range(8):
        line = taps[k:k + 1, :]
        hit = jnp.bitwise_and(line, 7) == sub
        value = jnp.where(hit, wts[k:k + 1, :], value)
        block = jnp.where(hit, lax.shift_right_logical(line, 3).astype(F32), block)
    ptap[...] = jnp.concatenate([value, block], axis=0).astype(BF16)

    @pl.loop(0, lines // CHUNK)
    def _(c):
        mapt[c] = vol[:, pl.ds(pl.multiple_of(c * CHUNK, CHUNK), CHUNK)].astype(BF16)

    pl.semaphore_wait(barrier, len(everyone))
    sends = []

    def go(copy, needed=None):
        if needed is None:
            copy.start()
        else:
            pl.when(needed)(copy.start)
        sends.append((copy, needed))
        return copy

    tap_copies = [go(remote(ptap, otap.at[p], tap_s.at[p], tap_r.at[p], peers[p])) for p in range(n_slab - 1)]
    x_copies = [
        [
            go(remote(mapt.at[c], omap.at[p, c], x_s.at[p, i], x_r.at[p, i], peers[p]))
            for i, c in enumerate([g * quarter + u for g in (mine_q, diag_q) for u in range(quarter)])
        ]
        for p in range(n_slab - 1)
    ]
    y_copies = [[None] * quarter for p in range(n_slab - 1)]
    z_copies = [[None] * quarter for p in range(n_slab - 1)]

    def forward(u):
        for p in range(n_slab - 1):
            x_copies[p][u].wait_recv()
            slot = omap.at[p, mine_q * quarter + u]
            y_copies[p][u] = go(remote(slot, slot, y_s.at[p, u], y_r.at[p, u], pair))
            z_copies[p][u] = go(remote(slot, slot, z_s.at[p, u], z_r.at[p, u], zpair))

    build_matrix(ptap, wide)
    forward(0)

    @pl.loop(0, rows // 256)
    def _(n):
        tile = pl.ds(pl.multiple_of(n * 256, 256), 256)
        work[:, tile] = img[:, tile].astype(F32)
        maps = jnp.concatenate([mapt[c] for c in range(4 * quarter)], axis=1)
        proj[:, tile] = jnp.dot(maps, wide[:, tile], preferred_element_type=F32)

    for u in range(1, quarter):
        forward(u)

    lane = lax.broadcasted_iota(jnp.int32, (1, rows), 1)
    who = lane // LPI
    focus = jnp.zeros((1, rows), F32)
    shift_x = jnp.zeros((1, rows), F32)
    shift_y = jnp.zeros((1, rows), F32)
    for p in range(rows // LPI):
        mine = who == p
        focus = jnp.where(mine, dfc[cls[0, p]], focus)
        shift_x = jnp.where(mine, shf[0, 0, p].astype(F32), shift_x)
        shift_y = jnp.where(mine, shf[0, 1, p].astype(F32), shift_y)
    theta = (lane - who * LPI).astype(F32) * (math.pi / LPI)
    along = shift_x * sine(theta + 0.5 * math.pi) + shift_y * sine(theta)
    turn = along * (math.pi / radii)
    subf = sub.astype(F32)
    first = subf * turn
    start_re, start_im = sine(first + 0.5 * math.pi), sine(first)
    eighth = 8.0 * turn
    turn_re, turn_im = sine(eighth + 0.5 * math.pi), sine(eighth)

    def phase_step(q, carry):
        e_re, e_im = carry
        re_rows = pl.ds(pl.multiple_of(8 * q, 8), 8)
        im_rows = pl.ds(pl.multiple_of(radii + 8 * q, 8), 8)
        ratio = (subf + (8 * q).astype(F32)) / radii
        ctf = -sine(CTF_GAIN * focus * (ratio * ratio) + PHASE_ZERO)
        im_re, im_im = work[re_rows, :], work[im_rows, :]
        work[re_rows, :] = ctf * (e_re * im_re + e_im * im_im)
        work[im_rows, :] = ctf * (e_re * im_im - e_im * im_re)
        c2 = ctf * ctf
        square[re_rows, :] = c2
        square[im_rows, :] = c2
        return e_re * turn_re - e_im * turn_im, e_re * turn_im + e_im * turn_re

    lax.fori_loop(0, radii // 8, phase_step, (start_re, start_im))

    for p in range(n_slab - 1):
        tap_copies[p].wait_recv()
        build_matrix(otap.at[p], owide)
        for g, copies in (
            (mine_q, []), (y_q, y_copies[p]), (z_q, z_copies[p]), (diag_q, x_copies[p][quarter:])
        ):
            for copy in copies:
                copy.wait_recv()
            depth = quarter * CHUNK
            deep = pl.ds(pl.multiple_of(g * depth, depth), depth)
            maps = jnp.concatenate([omap[p, g * quarter + u] for u in range(quarter)], axis=1)

            @pl.loop(0, rows // 256)
            def _(n):
                tile = pl.ds(pl.multiple_of(n * 256, 256), 256)
                proj[:, tile] += jnp.dot(maps, owide[deep, tile], preferred_element_type=F32)

    @pl.loop(0, cols // 16)
    def _(q):
        at = pl.ds(pl.multiple_of(16 * q, 16), 16)
        back[at, :] = (square[at, :] * proj[at, :] - work[at, :]).astype(BF16)

    def grad_block(b):
        return mul_nt(back[...], wide[pl.ds(pl.multiple_of(b * bw, bw), bw), :])

    middle = cols // 32 * 16
    parts = ((0, middle), (middle, cols - middle))
    spans = [pl.ds(*part) for part in parts]
    p_copies = []
    for t in range(nz):
        s1send[t] = grad_block(2 * zs[t] + 1 - y).astype(BF16)
        p_copies.append([
            go(remote(s1send.at[t, span, :], s1recv.at[t, span, :], p_s.at[t, u], p_r.at[t, u], pair))
            for u, span in enumerate(spans)
        ])
    q_copies = []
    for t in range(nz - 1):
        gown[t] = grad_block(2 * zs[t] + y)
        for u, span in enumerate(spans):
            p_copies[t][u].wait_recv()
            s2send[t, span, :] = (gown[t, span, :] + s1recv[t, span, :].astype(F32)).astype(BF16)
            q_copies.append(
                go(remote(s2send.at[t, span, :], s2recv.at[t, span, :], q_s.at[t, u], q_r.at[t, u], zpeers[t]))
            )
    gown[nz - 1] = grad_block(2 * zs[nz - 1] + y)
    for copy in p_copies[nz - 1]:
        copy.wait_recv()
    total = gown[nz - 1] + s1recv[nz - 1].astype(F32)
    for copy in q_copies:
        copy.wait_recv()
    for t in range(nz - 1):
        total = total + s2recv[t].astype(F32)
    gall[d] = total.astype(BF16)

    to_right, to_left = (h, d + 2, s), (h, d - 2, s)

    def share(zz, u):
        return gall.at[2 * zz + y, spans[u], :]

    def relay(k, u):
        for way, where, source, needed in (
            (0, to_right, z - k, jnp.logical_and(z - k >= 0, z + 1 < nz)),
            (1, to_left, z + k, jnp.logical_and(z + k < nz, z >= 1)),
        ):
            part = share(source, u)
            go(remote(part, part, g_s.at[way, k, u], g_r.at[way, k, u], where), needed)

    def from_pair(way, k, u, source, needed):
        part = share(source, u)
        pair_copies.append((go(remote(part, part, f_s.at[way, k, u], f_r.at[way, k, u], pair), needed), needed))

    pair_copies = []
    for u in range(2):
        relay(0, u)
        from_pair(0, 0, u, z, None)

    def arrive(k):
        for u in range(2):
            for way, source, needed in ((0, z - k, z - k >= 0), (1, z + k, z + k < nz)):
                part = share(source, u)
                come = remote(part, part, g_s.at[way, k - 1, u], g_r.at[way, k - 1, u], pair)
                pl.when(needed)(come.wait_recv)
                from_pair(way, k, u, source, needed)
            if k < nz - 1:
                relay(k, u)

    if bw % CHUNK == 0:
        mine = vol[:, pl.ds(pl.multiple_of(d * bw, CHUNK), bw)]
    else:
        at = (d * bw) // CHUNK
        near = vol[:, pl.ds(pl.multiple_of(at * CHUNK, CHUNK), CHUNK)]
        high = near.astype(BF16)
        low = (near - high.astype(F32)).astype(BF16)
        pick = placing(bw, d * bw - at * CHUNK)
        mine = mul_nt(high, pick) + mul_nt(low, pick)
    cand_wide = mine - step * total
    cand[...] = cand_wide.astype(BF16)
    c_copy = go(remote(cand, ocand, c_s.at[0], c_r.at[0], other_half))
    c_copy.wait_recv()
    theirs = ocand[...].astype(F32)

    def shell(a, b):
        prod = a * b
        prod = prod[:radii] + prod[radii:]
        return mul_nt(jnp.ones((8, bw), F32), prod, lax.Precision.HIGHEST)

    kind = lax.broadcasted_iota(jnp.int32, (8, radii), 0)
    den_mine, den_other = shell(cand_wide, cand_wide), shell(theirs, theirs)
    fs[0] = jnp.where(kind == 0, shell(cand_wide, theirs), jnp.where(kind == 1, den_mine, den_other))
    ux = [go(remote(fs.at[0], fx.at[p], ux_s.at[p], ux_r.at[p], peers[p])) for p in range(n_slab - 1)]

    arrive(1)
    sums = fs[0]
    for p in range(n_slab - 1):
        ux[p].wait_recv()
        sums = sums + fx[p]
    fs[1] = sums
    uy = go(remote(fs.at[1], fy, uy_s.at[0], uy_r.at[0], pair))
    if nz > 2:
        arrive(2)
    uy.wait_recv()
    sums = sums + fy[...]
    fs[2] = sums
    uz = [go(remote(fs.at[2], fz.at[t], uz_s.at[t], uz_r.at[t], zpeers[t])) for t in range(nz - 1)]
    for k in range(3, nz):
        arrive(k)
    for t in range(nz - 1):
        uz[t].wait_recv()
        sums = sums + fz[t]
    num, den_mine, den_other = sums[0:1], sums[1:2], sums[2:3]
    fsc = num / (jnp.sqrt(den_mine * den_other) + 1e-06)
    factor = step * (1.0 + fsc) / 2.0
    column = jnp.sum(eye(radii, F32) * factor, axis=1, keepdims=True)
    column = jnp.concatenate([column, column], axis=0)

    for copy, needed in pair_copies:
        if needed is None:
            copy.wait_recv()
        else:
            pl.when(needed)(copy.wait_recv)
    if bw % CHUNK == 0:
        for b in range(n_dom):
            out[:, b * bw:(b + 1) * bw] = column * gall[b].astype(F32)
    else:
        fold = CHUNK // bw

        @pl.loop(0, lines // CHUNK)
        def _(c):
            whole = jnp.zeros((cols, CHUNK), F32)
            for u in range(fold):
                whole = whole + jnp.dot(gall[c * fold + u], placing(bw, u * bw), preferred_element_type=F32)
            out[:, pl.ds(pl.multiple_of(c * CHUNK, CHUNK), CHUNK)] = column * whole

    for copy, needed in sends:
        if needed is None:
            copy.wait_send()
        else:
            pl.when(needed)(copy.wait_send)


def body(n_dom, n_slab, volume, images, tap_index, tap_weight, classes, shifts, defocus):
    slab_map, data = volume[0].T, images[0].T
    cols, lines = slab_map.shape
    rows = data.shape[1]
    depth = tap_index.shape[2]
    step = STEP_SCALE / math.sqrt(rows * n_dom * depth / lines)
    nz, bw = n_dom // 2, lines // n_dom
    nc, np_, nq = lines // CHUNK, n_slab - 1, lines // CHUNK // 4
    dma = pltpu.SemaphoreType.DMA
    vmem = pl.BlockSpec(memory_space=pltpu.VMEM)
    smem = pl.BlockSpec(memory_space=pltpu.SMEM)
    scratch = [
        pltpu.VMEM((nc, cols, CHUNK), BF16),
        pltpu.VMEM((np_, nc, cols, CHUNK), BF16),
        pltpu.VMEM((16, rows), BF16),
        pltpu.VMEM((np_, 16, rows), BF16),
        pltpu.VMEM((lines, rows), BF16),
        pltpu.VMEM((lines, rows), BF16),
        pltpu.VMEM((cols, rows), F32),
        pltpu.VMEM((cols, rows), F32),
        pltpu.VMEM((cols, rows), F32),
        pltpu.VMEM((cols, rows), BF16),
        pltpu.VMEM((nz, cols, bw), F32),
        pltpu.VMEM((nz, cols, bw), BF16),
        pltpu.VMEM((nz, cols, bw), BF16),
        pltpu.VMEM((nz - 1, cols, bw), BF16),
        pltpu.VMEM((nz - 1, cols, bw), BF16),
        pltpu.VMEM((n_dom, cols, bw), BF16),
        pltpu.VMEM((cols, bw), BF16),
        pltpu.VMEM((cols, bw), BF16),
        pltpu.VMEM((3, 8, cols // 2), F32),
        pltpu.VMEM((np_, 8, cols // 2), F32),
        pltpu.VMEM((8, cols // 2), F32),
        pltpu.VMEM((nz - 1, 8, cols // 2), F32),
    ]
    for shape in (
        (np_,), (np_, 2 * nq), (np_, nq), (np_, nq), (nz, 2), (nz - 1, 2), (2, nz - 1, 2), (2, nz, 2), (1,), (np_,), (1,), (nz - 1,)
    ):
        scratch += [dma(shape), dma(shape)]
    change = pl.pallas_call(
        functools.partial(kernel, n_dom, n_slab, step),
        out_shape=jax.ShapeDtypeStruct((cols, lines), F32),
        in_specs=[vmem] * 4 + [smem] * 3,
        out_specs=vmem,
        scratch_shapes=scratch,
        compiler_params=pltpu.CompilerParams(
            collective_id=0, has_side_effects=True, vmem_limit_bytes=30 * 1024 * 1024
        ),
    )(slab_map, data, tap_index[0, 0], tap_weight[0, 0], classes, shifts, defocus)
    return (slab_map - change).T[None]


def solution(mesh):
    placed = (
        P("half", "slab", None),
        P("half", "dom", None),
        P("half", "slab", None, "dom"),
        P("half", "slab", None, "dom"),
        P("half", "dom"),
        P("half", None, "dom"),
        P(),
    )
    return jax.shard_map(
        functools.partial(body, mesh.shape["dom"], mesh.shape["slab"]),
        mesh=mesh, in_specs=placed, out_specs=P("half", "slab", None), check_vma=False,
    )
```

```python
import functools
import math

import jax
import jax.numpy as jnp
from jax import lax
from jax.experimental import pallas as pl
from jax.experimental.pallas import tpu as pltpu
from jax.sharding import PartitionSpec as P

LPI = 64
CTF_GAIN = 30.0
PHASE_ZERO = 0.1
STEP_SCALE = 0.5
CHUNK = 128
MESH = pl.DeviceIdType.MESH
F32 = jnp.float32
BF16 = jnp.bfloat16


def sine(x):
    turns = jnp.floor(x * (1.0 / math.pi) + 0.5)
    y = ((x - turns * 3.140625) - turns * 9.67502593994140625e-4) - turns * 1.509957990978376432e-7
    odd = turns - 2.0 * jnp.floor(turns * 0.5)
    y2 = y * y
    poly = -1.0 / 39916800.0
    for inverse in (1.0 / 362880.0, -1.0 / 5040.0, 1.0 / 120.0, -1.0 / 6.0, 1.0):
        poly = poly * y2 + inverse
    return (y * poly) * (1.0 - 2.0 * odd)


def mul_nt(a, b, precision=None):
    return lax.dot_general(
        a, b, (((1,), (1,)), ((), ())), preferred_element_type=F32, precision=precision
    )


def eye(n, kind):
    row = lax.broadcasted_iota(jnp.int32, (n, n), 0)
    col = lax.broadcasted_iota(jnp.int32, (n, n), 1)
    return jnp.where(row == col, 1.0, 0.0).astype(kind)


def placing(n, offset):
    row = lax.broadcasted_iota(jnp.int32, (n, CHUNK), 0)
    col = lax.broadcasted_iota(jnp.int32, (n, CHUNK), 1)
    return jnp.where(row + offset == col, 1.0, 0.0).astype(BF16)


def remote(src, dst, send, recv, where):
    return pltpu.make_async_remote_copy(
        src_ref=src, dst_ref=dst, send_sem=send, recv_sem=recv, device_id=where, device_id_type=MESH
    )


def build_matrix(taps_ref, wide_ref):
    packed = taps_ref[...].astype(F32)
    value = jnp.concatenate([packed[:8], packed[:8]], axis=0)
    block = jnp.concatenate([packed[8:], packed[8:] - 1.0], axis=0)

    @pl.loop(0, wide_ref.shape[0] // 32)
    def _(t):
        for u in range(2):
            b = (4 * t + 2 * u).astype(F32)
            rows = pl.ds(pl.multiple_of(t * 32 + 16 * u, 16), 16)
            wide_ref[rows, :] = jnp.where(block == b, value, 0.0).astype(BF16)


def kernel(
    n_dom, n_slab, step,
    vol_hbm, img_hbm, taps_hbm, wts_hbm, cls_hbm, shf_hbm, dfc_hbm,
    out,
    vol, img, taps, wts, cls, shf, dfc,
    mapt, omap, ptap, otap, wide, owide, work, proj, square, back,
    gown, s1send, s1recv, s2send, s2recv, gall, cand, ocand, fs, fx, fy, fz,
    tap_s, tap_r, x_s, x_r, y_s, y_r, z_s, z_r, p_s, p_r, q_s, q_r, g_s, g_r, f_s, f_r, c_s, c_r,
    ux_s, ux_r, uy_s, uy_r, uz_s, uz_r, in_s,
):
    h, d, s = lax.axis_index("half"), lax.axis_index("dom"), lax.axis_index("slab")
    cols, lines = vol.shape
    radii = cols // 2
    rows = img.shape[1]
    nz = n_dom // 2
    y, z = lax.rem(d, 2), d // 2
    pair = (h, d + 1 - 2 * y, s)
    other_half = (1 - h, d, s)
    peers = [(h, d, lax.rem(s + p, n_slab)) for p in range(1, n_slab)]
    zs = [lax.rem(z + 1 + t, nz) for t in range(nz)]
    zpeers = [(h, 2 * zs[t] + y, s) for t in range(nz - 1)]
    bw = lines // n_dom
    quarter = lines // CHUNK // 4
    zpair = (h, d + 2 - 4 * lax.rem(z, 2), s)
    mine_q = 2 * lax.rem(z, 2) + y
    y_q, z_q, diag_q = mine_q + 1 - 2 * y, mine_q + 2 - 4 * lax.rem(z, 2), 3 - mine_q

    barrier = pltpu.get_barrier_semaphore()
    everyone = [pair, other_half] + peers + zpeers
    for who in everyone:
        pl.semaphore_signal(barrier, inc=1, device_id=who, device_id_type=MESH)

    pairs_in = (
        (taps_hbm, taps), (wts_hbm, wts), (vol_hbm, vol), (img_hbm, img),
        (cls_hbm, cls), (shf_hbm, shf), (dfc_hbm, dfc),
    )
    inputs = [pltpu.make_async_copy(src, dst, in_s.at[i]) for i, (src, dst) in enumerate(pairs_in)]
    for copy in inputs:
        copy.start()
    inputs[0].wait()
    inputs[1].wait()

    sub = lax.broadcasted_iota(jnp.int32, (8, rows), 0)
    value = jnp.zeros((8, rows), F32)
    block = jnp.zeros((8, rows), F32)
    for k in range(8):
        line = taps[k:k + 1, :]
        hit = jnp.bitwise_and(line, 7) == sub
        value = jnp.where(hit, wts[k:k + 1, :], value)
        block = jnp.where(hit, lax.shift_right_logical(line, 3).astype(F32), block)
    ptap[...] = jnp.concatenate([value, block], axis=0).astype(BF16)

    inputs[2].wait()

    @pl.loop(0, lines // CHUNK)
    def _(c):
        mapt[c] = vol[:, pl.ds(pl.multiple_of(c * CHUNK, CHUNK), CHUNK)].astype(BF16)

    pl.semaphore_wait(barrier, len(everyone))
    sends = []

    def go(copy, needed=None):
        if needed is None:
            copy.start()
        else:
            pl.when(needed)(copy.start)
        sends.append((copy, needed))
        return copy

    tap_copies = [go(remote(ptap, otap.at[p], tap_s.at[p], tap_r.at[p], peers[p])) for p in range(n_slab - 1)]
    x_copies = [
        [
            go(remote(mapt.at[c], omap.at[p, c], x_s.at[p, i], x_r.at[p, i], peers[p]))
            for i, c in enumerate([g * quarter + u for g in (mine_q, diag_q) for u in range(quarter)])
        ]
        for p in range(n_slab - 1)
    ]
    y_copies = [[None] * quarter for p in range(n_slab - 1)]
    z_copies = [[None] * quarter for p in range(n_slab - 1)]

    def forward(u):
        for p in range(n_slab - 1):
            x_copies[p][u].wait_recv()
            slot = omap.at[p, mine_q * quarter + u]
            y_copies[p][u] = go(remote(slot, slot, y_s.at[p, u], y_r.at[p, u], pair))
            z_copies[p][u] = go(remote(slot, slot, z_s.at[p, u], z_r.at[p, u], zpair))

    for copy in inputs[3:]:
        copy.wait()

    build_matrix(ptap, wide)
    forward(0)

    @pl.loop(0, rows // 256)
    def _(n):
        tile = pl.ds(pl.multiple_of(n * 256, 256), 256)
        work[:, tile] = img[:, tile].astype(F32)
        maps = jnp.concatenate([mapt[c] for c in range(4 * quarter)], axis=1)
        proj[:, tile] = jnp.dot(maps, wide[:, tile], preferred_element_type=F32)

    for u in range(1, quarter):
        forward(u)

    lane = lax.broadcasted_iota(jnp.int32, (1, rows), 1)
    who = lane // LPI
    focus = jnp.zeros((1, rows), F32)
    shift_x = jnp.zeros((1, rows), F32)
    shift_y = jnp.zeros((1, rows), F32)
    for p in range(rows // LPI):
        mine = who == p
        focus = jnp.where(mine, dfc[cls[0, p]], focus)
        shift_x = jnp.where(mine, shf[0, 0, p].astype(F32), shift_x)
        shift_y = jnp.where(mine, shf[0, 1, p].astype(F32), shift_y)
    theta = (lane - who * LPI).astype(F32) * (math.pi / LPI)
    along = shift_x * sine(theta + 0.5 * math.pi) + shift_y * sine(theta)
    turn = along * (math.pi / radii)
    subf = sub.astype(F32)
    first = subf * turn
    start_re, start_im = sine(first + 0.5 * math.pi), sine(first)
    eighth = 8.0 * turn
    turn_re, turn_im = sine(eighth + 0.5 * math.pi), sine(eighth)

    def phase_step(q, carry):
        e_re, e_im = carry
        re_rows = pl.ds(pl.multiple_of(8 * q, 8), 8)
        im_rows = pl.ds(pl.multiple_of(radii + 8 * q, 8), 8)
        ratio = (subf + (8 * q).astype(F32)) / radii
        ctf = -sine(CTF_GAIN * focus * (ratio * ratio) + PHASE_ZERO)
        im_re, im_im = work[re_rows, :], work[im_rows, :]
        work[re_rows, :] = ctf * (e_re * im_re + e_im * im_im)
        work[im_rows, :] = ctf * (e_re * im_im - e_im * im_re)
        c2 = ctf * ctf
        square[re_rows, :] = c2
        square[im_rows, :] = c2
        return e_re * turn_re - e_im * turn_im, e_re * turn_im + e_im * turn_re

    lax.fori_loop(0, radii // 8, phase_step, (start_re, start_im))

    for p in range(n_slab - 1):
        tap_copies[p].wait_recv()
        build_matrix(otap.at[p], owide)
        for g, copies in (
            (mine_q, []), (y_q, y_copies[p]), (z_q, z_copies[p]), (diag_q, x_copies[p][quarter:])
        ):
            for copy in copies:
                copy.wait_recv()
            depth = quarter * CHUNK
            deep = pl.ds(pl.multiple_of(g * depth, depth), depth)
            maps = jnp.concatenate([omap[p, g * quarter + u] for u in range(quarter)], axis=1)

            @pl.loop(0, rows // 256)
            def _(n):
                tile = pl.ds(pl.multiple_of(n * 256, 256), 256)
                proj[:, tile] += jnp.dot(maps, owide[deep, tile], preferred_element_type=F32)

    @pl.loop(0, cols // 16)
    def _(q):
        at = pl.ds(pl.multiple_of(16 * q, 16), 16)
        back[at, :] = (square[at, :] * proj[at, :] - work[at, :]).astype(BF16)

    def grad_block(b):
        return mul_nt(back[...], wide[pl.ds(pl.multiple_of(b * bw, bw), bw), :])

    middle = cols // 32 * 16
    parts = ((0, middle), (middle, cols - middle))
    spans = [pl.ds(*part) for part in parts]
    p_copies = []
    for t in range(nz):
        s1send[t] = grad_block(2 * zs[t] + 1 - y).astype(BF16)
        p_copies.append([
            go(remote(s1send.at[t, span, :], s1recv.at[t, span, :], p_s.at[t, u], p_r.at[t, u], pair))
            for u, span in enumerate(spans)
        ])
    q_copies = []
    for t in range(nz - 1):
        gown[t] = grad_block(2 * zs[t] + y)
        for u, span in enumerate(spans):
            p_copies[t][u].wait_recv()
            s2send[t, span, :] = (gown[t, span, :] + s1recv[t, span, :].astype(F32)).astype(BF16)
            q_copies.append(
                go(remote(s2send.at[t, span, :], s2recv.at[t, span, :], q_s.at[t, u], q_r.at[t, u], zpeers[t]))
            )
    gown[nz - 1] = grad_block(2 * zs[nz - 1] + y)
    for copy in p_copies[nz - 1]:
        copy.wait_recv()
    total = gown[nz - 1] + s1recv[nz - 1].astype(F32)
    for copy in q_copies:
        copy.wait_recv()
    for t in range(nz - 1):
        total = total + s2recv[t].astype(F32)
    gall[d] = total.astype(BF16)

    to_right, to_left = (h, d + 2, s), (h, d - 2, s)

    def share(zz, u):
        return gall.at[2 * zz + y, spans[u], :]

    def relay(k, u):
        for way, where, source, needed in (
            (0, to_right, z - k, jnp.logical_and(z - k >= 0, z + 1 < nz)),
            (1, to_left, z + k, jnp.logical_and(z + k < nz, z >= 1)),
        ):
            part = share(source, u)
            go(remote(part, part, g_s.at[way, k, u], g_r.at[way, k, u], where), needed)

    def from_pair(way, k, u, source, needed):
        part = share(source, u)
        pair_copies.append((go(remote(part, part, f_s.at[way, k, u], f_r.at[way, k, u], pair), needed), needed))

    pair_copies = []
    for u in range(2):
        relay(0, u)
        from_pair(0, 0, u, z, None)

    def arrive(k):
        for u in range(2):
            for way, source, needed in ((0, z - k, z - k >= 0), (1, z + k, z + k < nz)):
                part = share(source, u)
                come = remote(part, part, g_s.at[way, k - 1, u], g_r.at[way, k - 1, u], pair)
                pl.when(needed)(come.wait_recv)
                from_pair(way, k, u, source, needed)
            if k < nz - 1:
                relay(k, u)

    if bw % CHUNK == 0:
        mine = vol[:, pl.ds(pl.multiple_of(d * bw, CHUNK), bw)]
    else:
        at = (d * bw) // CHUNK
        near = vol[:, pl.ds(pl.multiple_of(at * CHUNK, CHUNK), CHUNK)]
        high = near.astype(BF16)
        low = (near - high.astype(F32)).astype(BF16)
        pick = placing(bw, d * bw - at * CHUNK)
        mine = mul_nt(high, pick) + mul_nt(low, pick)
    cand_wide = mine - step * total
    cand[...] = cand_wide.astype(BF16)
    c_copy = go(remote(cand, ocand, c_s.at[0], c_r.at[0], other_half))
    c_copy.wait_recv()
    theirs = ocand[...].astype(F32)

    def shell(a, b):
        prod = a * b
        prod = prod[:radii] + prod[radii:]
        return mul_nt(jnp.ones((8, bw), F32), prod, lax.Precision.HIGHEST)

    kind = lax.broadcasted_iota(jnp.int32, (8, radii), 0)
    den_mine, den_other = shell(cand_wide, cand_wide), shell(theirs, theirs)
    fs[0] = jnp.where(kind == 0, shell(cand_wide, theirs), jnp.where(kind == 1, den_mine, den_other))
    ux = [go(remote(fs.at[0], fx.at[p], ux_s.at[p], ux_r.at[p], peers[p])) for p in range(n_slab - 1)]

    arrive(1)
    sums = fs[0]
    for p in range(n_slab - 1):
        ux[p].wait_recv()
        sums = sums + fx[p]
    fs[1] = sums
    uy = go(remote(fs.at[1], fy, uy_s.at[0], uy_r.at[0], pair))
    if nz > 2:
        arrive(2)
    uy.wait_recv()
    sums = sums + fy[...]
    fs[2] = sums
    uz = [go(remote(fs.at[2], fz.at[t], uz_s.at[t], uz_r.at[t], zpeers[t])) for t in range(nz - 1)]
    for k in range(3, nz):
        arrive(k)
    for t in range(nz - 1):
        uz[t].wait_recv()
        sums = sums + fz[t]
    num, den_mine, den_other = sums[0:1], sums[1:2], sums[2:3]
    fsc = num / (jnp.sqrt(den_mine * den_other) + 1e-06)
    factor = step * (1.0 + fsc) / 2.0
    column = jnp.sum(eye(radii, F32) * factor, axis=1, keepdims=True)
    column = jnp.concatenate([column, column], axis=0)

    for copy, needed in pair_copies:
        if needed is None:
            copy.wait_recv()
        else:
            pl.when(needed)(copy.wait_recv)
    if bw % CHUNK == 0:
        for b in range(n_dom):
            out[:, b * bw:(b + 1) * bw] = (column * gall[b].astype(F32)).astype(BF16)
    else:
        fold = CHUNK // bw

        @pl.loop(0, lines // CHUNK)
        def _(c):
            whole = jnp.zeros((cols, CHUNK), F32)
            for u in range(fold):
                whole = whole + jnp.dot(gall[c * fold + u], placing(bw, u * bw), preferred_element_type=F32)
            out[:, pl.ds(pl.multiple_of(c * CHUNK, CHUNK), CHUNK)] = (column * whole).astype(BF16)

    for copy, needed in sends:
        if needed is None:
            copy.wait_send()
        else:
            pl.when(needed)(copy.wait_send)


def body(n_dom, n_slab, volume, images, tap_index, tap_weight, classes, shifts, defocus):
    slab_map, data = volume[0].T, images[0].T
    cols, lines = slab_map.shape
    rows = data.shape[1]
    depth = tap_index.shape[2]
    step = STEP_SCALE / math.sqrt(rows * n_dom * depth / lines)
    nz, bw = n_dom // 2, lines // n_dom
    nc, np_, nq = lines // CHUNK, n_slab - 1, lines // CHUNK // 4
    dma = pltpu.SemaphoreType.DMA
    vmem = pl.BlockSpec(memory_space=pltpu.VMEM)
    scratch = [
        pltpu.VMEM((cols, lines), F32),
        pltpu.VMEM((cols, rows), BF16),
        pltpu.VMEM(tap_index.shape[2:], jnp.int32),
        pltpu.VMEM(tap_weight.shape[2:], F32),
        pltpu.SMEM(classes.shape, jnp.int32),
        pltpu.SMEM(shifts.shape, jnp.int32),
        pltpu.SMEM(defocus.shape, F32),
        pltpu.VMEM((nc, cols, CHUNK), BF16),
        pltpu.VMEM((np_, nc, cols, CHUNK), BF16),
        pltpu.VMEM((16, rows), BF16),
        pltpu.VMEM((np_, 16, rows), BF16),
        pltpu.VMEM((lines, rows), BF16),
        pltpu.VMEM((lines, rows), BF16),
        pltpu.VMEM((cols, rows), F32),
        pltpu.VMEM((cols, rows), F32),
        pltpu.VMEM((cols, rows), F32),
        pltpu.VMEM((cols, rows), BF16),
        pltpu.VMEM((nz, cols, bw), F32),
        pltpu.VMEM((nz, cols, bw), BF16),
        pltpu.VMEM((nz, cols, bw), BF16),
        pltpu.VMEM((nz - 1, cols, bw), BF16),
        pltpu.VMEM((nz - 1, cols, bw), BF16),
        pltpu.VMEM((n_dom, cols, bw), BF16),
        pltpu.VMEM((cols, bw), BF16),
        pltpu.VMEM((cols, bw), BF16),
        pltpu.VMEM((3, 8, cols // 2), F32),
        pltpu.VMEM((np_, 8, cols // 2), F32),
        pltpu.VMEM((8, cols // 2), F32),
        pltpu.VMEM((nz - 1, 8, cols // 2), F32),
    ]
    for shape in (
        (np_,), (np_, 2 * nq), (np_, nq), (np_, nq), (nz, 2), (nz - 1, 2), (2, nz - 1, 2), (2, nz, 2), (1,), (np_,), (1,), (nz - 1,)
    ):
        scratch += [dma(shape), dma(shape)]
    scratch.append(dma((7,)))
    change = pl.pallas_call(
        functools.partial(kernel, n_dom, n_slab, step),
        out_shape=jax.ShapeDtypeStruct((cols, lines), BF16),
        in_specs=[pl.BlockSpec(memory_space=pltpu.HBM)] * 7,
        out_specs=vmem,
        scratch_shapes=scratch,
        compiler_params=pltpu.CompilerParams(
            collective_id=0, has_side_effects=True, vmem_limit_bytes=60 * 1024 * 1024
        ),
    )(slab_map, data, tap_index[0, 0], tap_weight[0, 0], classes, shifts, defocus)
    return (slab_map - change.astype(F32)).T[None]


def solution(mesh):
    placed = (
        P("half", "slab", None),
        P("half", "dom", None),
        P("half", "slab", None, "dom"),
        P("half", "slab", None, "dom"),
        P("half", "dom"),
        P("half", None, "dom"),
        P(),
    )
    return jax.shard_map(
        functools.partial(body, mesh.shape["dom"], mesh.shape["slab"]),
        mesh=mesh, in_specs=placed, out_specs=P("half", "slab", None), check_vma=False,
    )
```

```python
import functools
import math

import jax
import jax.numpy as jnp
from jax import lax
from jax.experimental import pallas as pl
from jax.experimental.pallas import tpu as pltpu
from jax.sharding import PartitionSpec as P

LPI = 64
CTF_GAIN = 30.0
PHASE_ZERO = 0.1
STEP_SCALE = 0.5
CHUNK = 128
MESH = pl.DeviceIdType.MESH
F32 = jnp.float32
BF16 = jnp.bfloat16


def sine(x):
    turns = jnp.floor(x * (1.0 / math.pi) + 0.5)
    y = ((x - turns * 3.140625) - turns * 9.67502593994140625e-4) - turns * 1.509957990978376432e-7
    odd = turns - 2.0 * jnp.floor(turns * 0.5)
    y2 = y * y
    poly = -1.0 / 39916800.0
    for inverse in (1.0 / 362880.0, -1.0 / 5040.0, 1.0 / 120.0, -1.0 / 6.0, 1.0):
        poly = poly * y2 + inverse
    return (y * poly) * (1.0 - 2.0 * odd)


def mul_nt(a, b, precision=None):
    return lax.dot_general(
        a, b, (((1,), (1,)), ((), ())), preferred_element_type=F32, precision=precision
    )


def eye(n, kind):
    row = lax.broadcasted_iota(jnp.int32, (n, n), 0)
    col = lax.broadcasted_iota(jnp.int32, (n, n), 1)
    return jnp.where(row == col, 1.0, 0.0).astype(kind)


def placing(n, offset):
    row = lax.broadcasted_iota(jnp.int32, (n, CHUNK), 0)
    col = lax.broadcasted_iota(jnp.int32, (n, CHUNK), 1)
    return jnp.where(row + offset == col, 1.0, 0.0).astype(BF16)


def remote(src, dst, send, recv, where):
    return pltpu.make_async_remote_copy(
        src_ref=src, dst_ref=dst, send_sem=send, recv_sem=recv, device_id=where, device_id_type=MESH
    )


def build_matrix(taps_ref, wide_ref):
    packed = taps_ref[...].astype(F32)
    value = jnp.concatenate([packed[:8], packed[:8]], axis=0)
    block = jnp.concatenate([packed[8:], packed[8:] - 1.0], axis=0)

    @pl.loop(0, wide_ref.shape[0] // 32)
    def _(t):
        for u in range(2):
            b = (4 * t + 2 * u).astype(F32)
            rows = pl.ds(pl.multiple_of(t * 32 + 16 * u, 16), 16)
            wide_ref[rows, :] = jnp.where(block == b, value, 0.0).astype(BF16)


def kernel(
    n_dom, n_slab, step,
    vol_hbm, img_hbm, taps_hbm, wts_hbm, cls_hbm, shf_hbm, dfc_hbm,
    out,
    vol, img, taps, wts, cls, shf, dfc,
    mapt, omap, ptap, otap, wide, owide, work, proj, square, back,
    gown, s1send, s1recv, s2send, s2recv, gall, cand, ocand, fs, fx, fy, fz,
    tap_s, tap_r, x_s, x_r, y_s, y_r, z_s, z_r, p_s, p_r, q_s, q_r, g_s, g_r, f_s, f_r, c_s, c_r,
    ux_s, ux_r, uy_s, uy_r, uz_s, uz_r, in_s,
):
    h, d, s = lax.axis_index("half"), lax.axis_index("dom"), lax.axis_index("slab")
    cols, lines = vol.shape
    radii = cols // 2
    rows = img.shape[1]
    nz = n_dom // 2
    y, z = lax.rem(d, 2), d // 2
    pair = (h, d + 1 - 2 * y, s)
    other_half = (1 - h, d, s)
    peers = [(h, d, lax.rem(s + p, n_slab)) for p in range(1, n_slab)]
    zs = [lax.rem(z + 1 + t, nz) for t in range(nz)]
    zpeers = [(h, 2 * zs[t] + y, s) for t in range(nz - 1)]
    bw = lines // n_dom
    quarter = lines // CHUNK // 4
    zpair = (h, d + 2 - 4 * lax.rem(z, 2), s)
    mine_q = 2 * lax.rem(z, 2) + y
    y_q, z_q, diag_q = mine_q + 1 - 2 * y, mine_q + 2 - 4 * lax.rem(z, 2), 3 - mine_q

    barrier = pltpu.get_barrier_semaphore()
    everyone = [pair, other_half] + peers + zpeers
    for who in everyone:
        pl.semaphore_signal(barrier, inc=1, device_id=who, device_id_type=MESH)

    pairs_in = (
        (taps_hbm, taps), (wts_hbm, wts), (vol_hbm, vol), (img_hbm, img),
        (cls_hbm, cls), (shf_hbm, shf), (dfc_hbm, dfc),
    )
    inputs = [pltpu.make_async_copy(src, dst, in_s.at[i]) for i, (src, dst) in enumerate(pairs_in)]
    for copy in inputs:
        copy.start()
    inputs[0].wait()
    inputs[1].wait()

    sub = lax.broadcasted_iota(jnp.int32, (8, rows), 0)
    value = jnp.zeros((8, rows), F32)
    block = jnp.zeros((8, rows), F32)
    for k in range(8):
        line = taps[k:k + 1, :]
        hit = jnp.bitwise_and(line, 7) == sub
        value = jnp.where(hit, wts[k:k + 1, :], value)
        block = jnp.where(hit, lax.shift_right_logical(line, 3).astype(F32), block)
    ptap[...] = jnp.concatenate([value, block], axis=0).astype(BF16)

    inputs[2].wait()

    @pl.loop(0, lines // CHUNK)
    def _(c):
        mapt[c] = vol[:, pl.ds(pl.multiple_of(c * CHUNK, CHUNK), CHUNK)].astype(BF16)

    pl.semaphore_wait(barrier, len(everyone))
    sends = []

    def go(copy, needed=None):
        if needed is None:
            copy.start()
        else:
            pl.when(needed)(copy.start)
        sends.append((copy, needed))
        return copy

    tap_copies = [go(remote(ptap, otap.at[p], tap_s.at[p], tap_r.at[p], peers[p])) for p in range(n_slab - 1)]
    x_copies = [
        [
            go(remote(mapt.at[c], omap.at[p, c], x_s.at[p, i], x_r.at[p, i], peers[p]))
            for i, c in enumerate([g * quarter + u for g in (mine_q, diag_q) for u in range(quarter)])
        ]
        for p in range(n_slab - 1)
    ]
    y_copies = [[None] * quarter for p in range(n_slab - 1)]
    z_copies = [[None] * quarter for p in range(n_slab - 1)]

    def forward(u):
        for p in range(n_slab - 1):
            x_copies[p][u].wait_recv()
            slot = omap.at[p, mine_q * quarter + u]
            y_copies[p][u] = go(remote(slot, slot, y_s.at[p, u], y_r.at[p, u], pair))
            z_copies[p][u] = go(remote(slot, slot, z_s.at[p, u], z_r.at[p, u], zpair))

    for copy in inputs[3:]:
        copy.wait()

    build_matrix(ptap, wide)
    forward(0)

    @pl.loop(0, rows // 256)
    def _(n):
        tile = pl.ds(pl.multiple_of(n * 256, 256), 256)
        work[:, tile] = img[:, tile].astype(F32)
        maps = jnp.concatenate([mapt[c] for c in range(4 * quarter)], axis=1)
        proj[:, tile] = jnp.dot(maps, wide[:, tile], preferred_element_type=F32)

    for u in range(1, quarter):
        forward(u)

    lane = lax.broadcasted_iota(jnp.int32, (1, rows), 1)
    who = lane // LPI
    focus = jnp.zeros((1, rows), F32)
    shift_x = jnp.zeros((1, rows), F32)
    shift_y = jnp.zeros((1, rows), F32)
    for p in range(rows // LPI):
        mine = who == p
        focus = jnp.where(mine, dfc[cls[0, p]], focus)
        shift_x = jnp.where(mine, shf[0, 0, p].astype(F32), shift_x)
        shift_y = jnp.where(mine, shf[0, 1, p].astype(F32), shift_y)
    theta = (lane - who * LPI).astype(F32) * (math.pi / LPI)
    along = shift_x * sine(theta + 0.5 * math.pi) + shift_y * sine(theta)
    turn = along * (math.pi / radii)
    subf = sub.astype(F32)
    first = subf * turn
    start_re, start_im = sine(first + 0.5 * math.pi), sine(first)
    eighth = 8.0 * turn
    turn_re, turn_im = sine(eighth + 0.5 * math.pi), sine(eighth)

    def phase_step(q, carry):
        e_re, e_im = carry
        re_rows = pl.ds(pl.multiple_of(8 * q, 8), 8)
        im_rows = pl.ds(pl.multiple_of(radii + 8 * q, 8), 8)
        ratio = (subf + (8 * q).astype(F32)) / radii
        ctf = -sine(CTF_GAIN * focus * (ratio * ratio) + PHASE_ZERO)
        im_re, im_im = work[re_rows, :], work[im_rows, :]
        work[re_rows, :] = ctf * (e_re * im_re + e_im * im_im)
        work[im_rows, :] = ctf * (e_re * im_im - e_im * im_re)
        c2 = ctf * ctf
        square[re_rows, :] = c2
        square[im_rows, :] = c2
        return e_re * turn_re - e_im * turn_im, e_re * turn_im + e_im * turn_re

    lax.fori_loop(0, radii // 8, phase_step, (start_re, start_im))

    for p in range(n_slab - 1):
        tap_copies[p].wait_recv()
        build_matrix(otap.at[p], owide)
        for g, copies in (
            (mine_q, []), (y_q, y_copies[p]), (z_q, z_copies[p]), (diag_q, x_copies[p][quarter:])
        ):
            for copy in copies:
                copy.wait_recv()
            depth = quarter * CHUNK
            deep = pl.ds(pl.multiple_of(g * depth, depth), depth)
            maps = jnp.concatenate([omap[p, g * quarter + u] for u in range(quarter)], axis=1)

            @pl.loop(0, rows // 256)
            def _(n):
                tile = pl.ds(pl.multiple_of(n * 256, 256), 256)
                proj[:, tile] += jnp.dot(maps, owide[deep, tile], preferred_element_type=F32)

    @pl.loop(0, cols // 16)
    def _(q):
        at = pl.ds(pl.multiple_of(16 * q, 16), 16)
        back[at, :] = (square[at, :] * proj[at, :] - work[at, :]).astype(BF16)

    def grad_block(b):
        return mul_nt(back[...], wide[pl.ds(pl.multiple_of(b * bw, bw), bw), :])

    middle = cols // 32 * 16
    parts = ((0, middle), (middle, cols - middle))
    spans = [pl.ds(*part) for part in parts]
    p_copies = []
    for t in range(nz):
        s1send[t] = grad_block(2 * zs[t] + 1 - y).astype(BF16)
        p_copies.append([
            go(remote(s1send.at[t, span, :], s1recv.at[t, span, :], p_s.at[t, u], p_r.at[t, u], pair))
            for u, span in enumerate(spans)
        ])
    q_copies = []
    for t in range(nz - 1):
        gown[t] = grad_block(2 * zs[t] + y)
        for u, span in enumerate(spans):
            p_copies[t][u].wait_recv()
            s2send[t, span, :] = (gown[t, span, :] + s1recv[t, span, :].astype(F32)).astype(BF16)
            q_copies.append(
                go(remote(s2send.at[t, span, :], s2recv.at[t, span, :], q_s.at[t, u], q_r.at[t, u], zpeers[t]))
            )
    gown[nz - 1] = grad_block(2 * zs[nz - 1] + y)
    for copy in p_copies[nz - 1]:
        copy.wait_recv()
    total = gown[nz - 1] + s1recv[nz - 1].astype(F32)
    for copy in q_copies:
        copy.wait_recv()
    for t in range(nz - 1):
        total = total + s2recv[t].astype(F32)
    gall[d] = total.astype(BF16)

    to_right, to_left = (h, d + 2, s), (h, d - 2, s)

    def share(zz, u):
        return gall.at[2 * zz + y, spans[u], :]

    def relay(k, u):
        for way, where, source, needed in (
            (0, to_right, z - k, jnp.logical_and(z - k >= 0, z + 1 < nz)),
            (1, to_left, z + k, jnp.logical_and(z + k < nz, z >= 1)),
        ):
            part = share(source, u)
            go(remote(part, part, g_s.at[way, k, u], g_r.at[way, k, u], where), needed)

    def from_pair(way, k, u, source, needed):
        part = share(source, u)
        pair_copies.append((go(remote(part, part, f_s.at[way, k, u], f_r.at[way, k, u], pair), needed), needed))

    pair_copies = []
    for u in range(2):
        relay(0, u)
        from_pair(0, 0, u, z, None)

    def arrive(k):
        for u in range(2):
            for way, source, needed in ((0, z - k, z - k >= 0), (1, z + k, z + k < nz)):
                part = share(source, u)
                come = remote(part, part, g_s.at[way, k - 1, u], g_r.at[way, k - 1, u], pair)
                pl.when(needed)(come.wait_recv)
            if k < nz - 1:
                relay(k, u)
            for way, source, needed in ((0, z - k, z - k >= 0), (1, z + k, z + k < nz)):
                from_pair(way, k, u, source, needed)

    if bw % CHUNK == 0:
        mine = vol[:, pl.ds(pl.multiple_of(d * bw, CHUNK), bw)]
    else:
        at = (d * bw) // CHUNK
        near = vol[:, pl.ds(pl.multiple_of(at * CHUNK, CHUNK), CHUNK)]
        high = near.astype(BF16)
        low = (near - high.astype(F32)).astype(BF16)
        pick = placing(bw, d * bw - at * CHUNK)
        mine = mul_nt(high, pick) + mul_nt(low, pick)
    cand_wide = mine - step * total
    cand[...] = cand_wide.astype(BF16)
    c_copy = go(remote(cand, ocand, c_s.at[0], c_r.at[0], other_half))
    c_copy.wait_recv()
    theirs = ocand[...].astype(F32)

    def shell(a, b):
        prod = a * b
        prod = prod[:radii] + prod[radii:]
        return mul_nt(jnp.ones((8, bw), F32), prod, lax.Precision.HIGHEST)

    kind = lax.broadcasted_iota(jnp.int32, (8, radii), 0)
    den_mine, den_other = shell(cand_wide, cand_wide), shell(theirs, theirs)
    fs[0] = jnp.where(kind == 0, shell(cand_wide, theirs), jnp.where(kind == 1, den_mine, den_other))
    ux = [go(remote(fs.at[0], fx.at[p], ux_s.at[p], ux_r.at[p], peers[p])) for p in range(n_slab - 1)]

    arrive(1)
    sums = fs[0]
    for p in range(n_slab - 1):
        ux[p].wait_recv()
        sums = sums + fx[p]
    fs[1] = sums
    uy = go(remote(fs.at[1], fy, uy_s.at[0], uy_r.at[0], pair))
    if nz > 2:
        arrive(2)
    uy.wait_recv()
    sums = sums + fy[...]
    fs[2] = sums
    uz = [go(remote(fs.at[2], fz.at[t], uz_s.at[t], uz_r.at[t], zpeers[t])) for t in range(nz - 1)]
    for k in range(3, nz):
        arrive(k)
    for t in range(nz - 1):
        uz[t].wait_recv()
        sums = sums + fz[t]
    num, den_mine, den_other = sums[0:1], sums[1:2], sums[2:3]
    fsc = num / (jnp.sqrt(den_mine * den_other) + 1e-06)
    factor = step * (1.0 + fsc) / 2.0
    column = jnp.sum(eye(radii, F32) * factor, axis=1, keepdims=True)
    column = jnp.concatenate([column, column], axis=0)

    for copy, needed in pair_copies:
        if needed is None:
            copy.wait_recv()
        else:
            pl.when(needed)(copy.wait_recv)
    if bw % CHUNK == 0:
        for b in range(n_dom):
            out[:, b * bw:(b + 1) * bw] = (column * gall[b].astype(F32)).astype(BF16)
    else:
        fold = CHUNK // bw

        @pl.loop(0, lines // CHUNK)
        def _(c):
            whole = jnp.zeros((cols, CHUNK), F32)
            for u in range(fold):
                whole = whole + jnp.dot(gall[c * fold + u], placing(bw, u * bw), preferred_element_type=F32)
            out[:, pl.ds(pl.multiple_of(c * CHUNK, CHUNK), CHUNK)] = (column * whole).astype(BF16)

    for copy, needed in sends:
        if needed is None:
            copy.wait_send()
        else:
            pl.when(needed)(copy.wait_send)


def body(n_dom, n_slab, volume, images, tap_index, tap_weight, classes, shifts, defocus):
    slab_map, data = volume[0].T, images[0].T
    cols, lines = slab_map.shape
    rows = data.shape[1]
    depth = tap_index.shape[2]
    step = STEP_SCALE / math.sqrt(rows * n_dom * depth / lines)
    nz, bw = n_dom // 2, lines // n_dom
    nc, np_, nq = lines // CHUNK, n_slab - 1, lines // CHUNK // 4
    dma = pltpu.SemaphoreType.DMA
    vmem = pl.BlockSpec(memory_space=pltpu.VMEM)
    scratch = [
        pltpu.VMEM((cols, lines), F32),
        pltpu.VMEM((cols, rows), BF16),
        pltpu.VMEM(tap_index.shape[2:], jnp.int32),
        pltpu.VMEM(tap_weight.shape[2:], F32),
        pltpu.SMEM(classes.shape, jnp.int32),
        pltpu.SMEM(shifts.shape, jnp.int32),
        pltpu.SMEM(defocus.shape, F32),
        pltpu.VMEM((nc, cols, CHUNK), BF16),
        pltpu.VMEM((np_, nc, cols, CHUNK), BF16),
        pltpu.VMEM((16, rows), BF16),
        pltpu.VMEM((np_, 16, rows), BF16),
        pltpu.VMEM((lines, rows), BF16),
        pltpu.VMEM((lines, rows), BF16),
        pltpu.VMEM((cols, rows), F32),
        pltpu.VMEM((cols, rows), F32),
        pltpu.VMEM((cols, rows), F32),
        pltpu.VMEM((cols, rows), BF16),
        pltpu.VMEM((nz, cols, bw), F32),
        pltpu.VMEM((nz, cols, bw), BF16),
        pltpu.VMEM((nz, cols, bw), BF16),
        pltpu.VMEM((nz - 1, cols, bw), BF16),
        pltpu.VMEM((nz - 1, cols, bw), BF16),
        pltpu.VMEM((n_dom, cols, bw), BF16),
        pltpu.VMEM((cols, bw), BF16),
        pltpu.VMEM((cols, bw), BF16),
        pltpu.VMEM((3, 8, cols // 2), F32),
        pltpu.VMEM((np_, 8, cols // 2), F32),
        pltpu.VMEM((8, cols // 2), F32),
        pltpu.VMEM((nz - 1, 8, cols // 2), F32),
    ]
    for shape in (
        (np_,), (np_, 2 * nq), (np_, nq), (np_, nq), (nz, 2), (nz - 1, 2), (2, nz - 1, 2), (2, nz, 2), (1,), (np_,), (1,), (nz - 1,)
    ):
        scratch += [dma(shape), dma(shape)]
    scratch.append(dma((7,)))
    change = pl.pallas_call(
        functools.partial(kernel, n_dom, n_slab, step),
        out_shape=jax.ShapeDtypeStruct((cols, lines), BF16),
        in_specs=[pl.BlockSpec(memory_space=pltpu.HBM)] * 7,
        out_specs=vmem,
        scratch_shapes=scratch,
        compiler_params=pltpu.CompilerParams(
            collective_id=0, has_side_effects=True, vmem_limit_bytes=60 * 1024 * 1024
        ),
    )(slab_map, data, tap_index[0, 0], tap_weight[0, 0], classes, shifts, defocus)
    return (slab_map - change.astype(F32)).T[None]


def solution(mesh):
    placed = (
        P("half", "slab", None),
        P("half", "dom", None),
        P("half", "slab", None, "dom"),
        P("half", "slab", None, "dom"),
        P("half", "dom"),
        P("half", None, "dom"),
        P(),
    )
    return jax.shard_map(
        functools.partial(body, mesh.shape["dom"], mesh.shape["slab"]),
        mesh=mesh, in_specs=placed, out_specs=P("half", "slab", None), check_vma=False,
    )
```

```python
import functools
import math

import jax
import jax.numpy as jnp
from jax import lax
from jax.experimental import pallas as pl
from jax.experimental.pallas import tpu as pltpu
from jax.sharding import PartitionSpec as P

LPI = 64
CTF_GAIN = 30.0
PHASE_ZERO = 0.1
STEP_SCALE = 0.5
CHUNK = 128
MESH = pl.DeviceIdType.MESH
F32 = jnp.float32
BF16 = jnp.bfloat16


def sine(x):
    turns = jnp.floor(x * (1.0 / math.pi) + 0.5)
    y = ((x - turns * 3.140625) - turns * 9.67502593994140625e-4) - turns * 1.509957990978376432e-7
    odd = turns - 2.0 * jnp.floor(turns * 0.5)
    y2 = y * y
    poly = -1.0 / 39916800.0
    for inverse in (1.0 / 362880.0, -1.0 / 5040.0, 1.0 / 120.0, -1.0 / 6.0, 1.0):
        poly = poly * y2 + inverse
    return (y * poly) * (1.0 - 2.0 * odd)


def mul_nt(a, b, precision=None):
    return lax.dot_general(
        a, b, (((1,), (1,)), ((), ())), preferred_element_type=F32, precision=precision
    )


def eye(n, kind):
    row = lax.broadcasted_iota(jnp.int32, (n, n), 0)
    col = lax.broadcasted_iota(jnp.int32, (n, n), 1)
    return jnp.where(row == col, 1.0, 0.0).astype(kind)


def placing(n, offset):
    row = lax.broadcasted_iota(jnp.int32, (n, CHUNK), 0)
    col = lax.broadcasted_iota(jnp.int32, (n, CHUNK), 1)
    return jnp.where(row + offset == col, 1.0, 0.0).astype(BF16)


def remote(src, dst, send, recv, where):
    return pltpu.make_async_remote_copy(
        src_ref=src, dst_ref=dst, send_sem=send, recv_sem=recv, device_id=where, device_id_type=MESH
    )


def build_matrix(taps_ref, wide_ref):
    packed = taps_ref[...].astype(F32)
    value = jnp.concatenate([packed[:8], packed[:8]], axis=0)
    block = jnp.concatenate([packed[8:], packed[8:] - 1.0], axis=0)

    @pl.loop(0, wide_ref.shape[0] // 32)
    def _(t):
        for u in range(2):
            b = (4 * t + 2 * u).astype(F32)
            rows = pl.ds(pl.multiple_of(t * 32 + 16 * u, 16), 16)
            wide_ref[rows, :] = jnp.where(block == b, value, 0.0).astype(BF16)


def kernel(
    n_dom, n_slab, step,
    vol_hbm, img_hbm, taps_hbm, wts_hbm, cls_hbm, shf_hbm, dfc_hbm,
    out,
    vol, img, taps, wts, cls, shf, dfc,
    mapt, omap, ptap, otap, wide, owide, work, proj, square, back,
    gown, s1send, s1recv, s2send, s2recv, gall, cand, ocand, fs, fx, fy, fz,
    tap_s, tap_r, x_s, x_r, y_s, y_r, z_s, z_r, p_s, p_r, q_s, q_r, g_s, g_r, f_s, f_r, c_s, c_r,
    ux_s, ux_r, uy_s, uy_r, uz_s, uz_r, e_s, e_r, in_s,
):
    h, d, s = lax.axis_index("half"), lax.axis_index("dom"), lax.axis_index("slab")
    cols, lines = vol.shape
    radii = cols // 2
    rows = img.shape[1]
    nz = n_dom // 2
    y, z = lax.rem(d, 2), d // 2
    pair = (h, d + 1 - 2 * y, s)
    other_half = (1 - h, d, s)
    peers = [(h, d, lax.rem(s + p, n_slab)) for p in range(1, n_slab)]
    zs = [lax.rem(z + 1 + t, nz) for t in range(nz)]
    zpeers = [(h, 2 * zs[t] + y, s) for t in range(nz - 1)]
    bw = lines // n_dom
    quarter = lines // CHUNK // 4
    zpair = (h, d + 2 - 4 * lax.rem(z, 2), s)
    mine_q = 2 * lax.rem(z, 2) + y
    y_q, z_q, diag_q = mine_q + 1 - 2 * y, mine_q + 2 - 4 * lax.rem(z, 2), 3 - mine_q

    barrier = pltpu.get_barrier_semaphore()
    everyone = [pair, other_half] + peers + zpeers
    for who in everyone:
        pl.semaphore_signal(barrier, inc=1, device_id=who, device_id_type=MESH)

    pairs_in = (
        (taps_hbm, taps), (wts_hbm, wts), (vol_hbm, vol), (img_hbm, img),
        (cls_hbm, cls), (shf_hbm, shf), (dfc_hbm, dfc),
    )
    inputs = [pltpu.make_async_copy(src, dst, in_s.at[i]) for i, (src, dst) in enumerate(pairs_in)]
    for copy in inputs:
        copy.start()
    inputs[0].wait()
    inputs[1].wait()

    sub = lax.broadcasted_iota(jnp.int32, (8, rows), 0)
    value = jnp.zeros((8, rows), F32)
    block = jnp.zeros((8, rows), F32)
    for k in range(8):
        line = taps[k:k + 1, :]
        hit = jnp.bitwise_and(line, 7) == sub
        value = jnp.where(hit, wts[k:k + 1, :], value)
        block = jnp.where(hit, lax.shift_right_logical(line, 3).astype(F32), block)
    ptap[...] = jnp.concatenate([value, block], axis=0).astype(BF16)

    inputs[2].wait()

    @pl.loop(0, lines // CHUNK)
    def _(c):
        mapt[c] = vol[:, pl.ds(pl.multiple_of(c * CHUNK, CHUNK), CHUNK)].astype(BF16)

    pl.semaphore_wait(barrier, len(everyone))
    sends = []

    def go(copy, needed=None):
        if needed is None:
            copy.start()
        else:
            pl.when(needed)(copy.start)
        sends.append((copy, needed))
        return copy

    tap_copies = [go(remote(ptap, otap.at[p], tap_s.at[p], tap_r.at[p], peers[p])) for p in range(n_slab - 1)]
    top, rest = pl.ds(0, cols // 32 * 16), pl.ds(cols // 32 * 16, cols - cols // 32 * 16)

    def held(ref, i):
        return ref.at[top, :] if i == quarter else ref

    x_copies = [
        [
            go(remote(held(mapt.at[c], i), held(omap.at[p, c], i), x_s.at[p, i], x_r.at[p, i], peers[p]))
            for i, c in enumerate([g * quarter + u for g in (mine_q, diag_q) for u in range(quarter)])
        ]
        for p in range(n_slab - 1)
    ]
    y_copies = [[None] * quarter for p in range(n_slab - 1)]
    z_copies = [[None] * quarter for p in range(n_slab - 1)]

    def forward(u):
        for p in range(n_slab - 1):
            x_copies[p][u].wait_recv()
            slot = omap.at[p, mine_q * quarter + u]
            y_copies[p][u] = go(remote(slot, slot, y_s.at[p, u], y_r.at[p, u], pair))
            z_copies[p][u] = go(remote(slot, slot, z_s.at[p, u], z_r.at[p, u], zpair))

    for copy in inputs[3:]:
        copy.wait()

    build_matrix(ptap, wide)
    forward(0)

    @pl.loop(0, rows // 256)
    def _(n):
        tile = pl.ds(pl.multiple_of(n * 256, 256), 256)
        work[:, tile] = img[:, tile].astype(F32)
        maps = jnp.concatenate([mapt[c] for c in range(4 * quarter)], axis=1)
        proj[:, tile] = jnp.dot(maps, wide[:, tile], preferred_element_type=F32)

    for u in range(1, quarter):
        forward(u)

    lane = lax.broadcasted_iota(jnp.int32, (1, rows), 1)
    who = lane // LPI
    focus = jnp.zeros((1, rows), F32)
    shift_x = jnp.zeros((1, rows), F32)
    shift_y = jnp.zeros((1, rows), F32)
    for p in range(rows // LPI):
        mine = who == p
        focus = jnp.where(mine, dfc[cls[0, p]], focus)
        shift_x = jnp.where(mine, shf[0, 0, p].astype(F32), shift_x)
        shift_y = jnp.where(mine, shf[0, 1, p].astype(F32), shift_y)
    theta = (lane - who * LPI).astype(F32) * (math.pi / LPI)
    along = shift_x * sine(theta + 0.5 * math.pi) + shift_y * sine(theta)
    turn = along * (math.pi / radii)
    subf = sub.astype(F32)
    first = subf * turn
    start_re, start_im = sine(first + 0.5 * math.pi), sine(first)
    eighth = 8.0 * turn
    turn_re, turn_im = sine(eighth + 0.5 * math.pi), sine(eighth)

    def phase_step(q, carry):
        e_re, e_im = carry
        re_rows = pl.ds(pl.multiple_of(8 * q, 8), 8)
        im_rows = pl.ds(pl.multiple_of(radii + 8 * q, 8), 8)
        ratio = (subf + (8 * q).astype(F32)) / radii
        ctf = -sine(CTF_GAIN * focus * (ratio * ratio) + PHASE_ZERO)
        im_re, im_im = work[re_rows, :], work[im_rows, :]
        work[re_rows, :] = ctf * (e_re * im_re + e_im * im_im)
        work[im_rows, :] = ctf * (e_re * im_im - e_im * im_re)
        c2 = ctf * ctf
        square[re_rows, :] = c2
        square[im_rows, :] = c2
        return e_re * turn_re - e_im * turn_im, e_re * turn_im + e_im * turn_re

    lax.fori_loop(0, radii // 8, phase_step, (start_re, start_im))
    extra = []
    for p in range(n_slab - 1):
        z_copies[p][0].wait_recv()
        slot = omap.at[p, z_q * quarter, rest, :]
        extra.append(go(remote(slot, slot, e_s.at[p], e_r.at[p], pair)))

    for p in range(n_slab - 1):
        tap_copies[p].wait_recv()
        build_matrix(otap.at[p], owide)
        for g, copies in (
            (mine_q, []), (y_q, y_copies[p]), (z_q, z_copies[p][1:]), (diag_q, x_copies[p][quarter:] + [extra[p]])
        ):
            for copy in copies:
                copy.wait_recv()
            depth = quarter * CHUNK
            deep = pl.ds(pl.multiple_of(g * depth, depth), depth)
            maps = jnp.concatenate([omap[p, g * quarter + u] for u in range(quarter)], axis=1)

            @pl.loop(0, rows // 256)
            def _(n):
                tile = pl.ds(pl.multiple_of(n * 256, 256), 256)
                proj[:, tile] += jnp.dot(maps, owide[deep, tile], preferred_element_type=F32)

    @pl.loop(0, cols // 16)
    def _(q):
        at = pl.ds(pl.multiple_of(16 * q, 16), 16)
        back[at, :] = (square[at, :] * proj[at, :] - work[at, :]).astype(BF16)

    def grad_block(b):
        return mul_nt(back[...], wide[pl.ds(pl.multiple_of(b * bw, bw), bw), :])

    middle = cols // 32 * 16
    parts = ((0, middle), (middle, cols - middle))
    spans = [pl.ds(*part) for part in parts]
    p_copies = []
    for t in range(nz):
        s1send[t] = grad_block(2 * zs[t] + 1 - y).astype(BF16)
        p_copies.append([
            go(remote(s1send.at[t, span, :], s1recv.at[t, span, :], p_s.at[t, u], p_r.at[t, u], pair))
            for u, span in enumerate(spans)
        ])
    q_copies = []
    for t in range(nz - 1):
        gown[t] = grad_block(2 * zs[t] + y)
        for u, span in enumerate(spans):
            p_copies[t][u].wait_recv()
            s2send[t, span, :] = (gown[t, span, :] + s1recv[t, span, :].astype(F32)).astype(BF16)
            q_copies.append(
                go(remote(s2send.at[t, span, :], s2recv.at[t, span, :], q_s.at[t, u], q_r.at[t, u], zpeers[t]))
            )
    gown[nz - 1] = grad_block(2 * zs[nz - 1] + y)
    for copy in p_copies[nz - 1]:
        copy.wait_recv()
    total = gown[nz - 1] + s1recv[nz - 1].astype(F32)
    for copy in q_copies:
        copy.wait_recv()
    for t in range(nz - 1):
        total = total + s2recv[t].astype(F32)
    gall[d] = total.astype(BF16)

    to_right, to_left = (h, d + 2, s), (h, d - 2, s)

    def share(zz, u):
        return gall.at[2 * zz + y, spans[u], :]

    def relay(k, u):
        for way, where, source, needed in (
            (0, to_right, z - k, jnp.logical_and(z - k >= 0, z + 1 < nz)),
            (1, to_left, z + k, jnp.logical_and(z + k < nz, z >= 1)),
        ):
            part = share(source, u)
            go(remote(part, part, g_s.at[way, k, u], g_r.at[way, k, u], where), needed)

    def from_pair(way, k, u, source, needed):
        part = share(source, u)
        pair_copies.append((go(remote(part, part, f_s.at[way, k, u], f_r.at[way, k, u], pair), needed), needed))

    pair_copies = []
    for u in range(2):
        relay(0, u)
        from_pair(0, 0, u, z, None)

    def arrive(k):
        for u in range(2):
            for way, source, needed in ((0, z - k, z - k >= 0), (1, z + k, z + k < nz)):
                part = share(source, u)
                come = remote(part, part, g_s.at[way, k - 1, u], g_r.at[way, k - 1, u], pair)
                pl.when(needed)(come.wait_recv)
                from_pair(way, k, u, source, needed)
            if k < nz - 1:
                relay(k, u)

    if bw % CHUNK == 0:
        mine = vol[:, pl.ds(pl.multiple_of(d * bw, CHUNK), bw)]
    else:
        at = (d * bw) // CHUNK
        near = vol[:, pl.ds(pl.multiple_of(at * CHUNK, CHUNK), CHUNK)]
        high = near.astype(BF16)
        low = (near - high.astype(F32)).astype(BF16)
        pick = placing(bw, d * bw - at * CHUNK)
        mine = mul_nt(high, pick) + mul_nt(low, pick)
    cand_wide = mine - step * total
    cand[...] = cand_wide.astype(BF16)
    c_copy = go(remote(cand, ocand, c_s.at[0], c_r.at[0], other_half))
    c_copy.wait_recv()
    theirs = ocand[...].astype(F32)

    def shell(a, b):
        prod = a * b
        prod = prod[:radii] + prod[radii:]
        return mul_nt(jnp.ones((8, bw), F32), prod, lax.Precision.HIGHEST)

    kind = lax.broadcasted_iota(jnp.int32, (8, radii), 0)
    den_mine, den_other = shell(cand_wide, cand_wide), shell(theirs, theirs)
    fs[0] = jnp.where(kind == 0, shell(cand_wide, theirs), jnp.where(kind == 1, den_mine, den_other))
    ux = [go(remote(fs.at[0], fx.at[p], ux_s.at[p], ux_r.at[p], peers[p])) for p in range(n_slab - 1)]

    arrive(1)
    sums = fs[0]
    for p in range(n_slab - 1):
        ux[p].wait_recv()
        sums = sums + fx[p]
    fs[1] = sums
    uy = go(remote(fs.at[1], fy, uy_s.at[0], uy_r.at[0], pair))
    if nz > 2:
        arrive(2)
    uy.wait_recv()
    sums = sums + fy[...]
    fs[2] = sums
    uz = [go(remote(fs.at[2], fz.at[t], uz_s.at[t], uz_r.at[t], zpeers[t])) for t in range(nz - 1)]
    for k in range(3, nz):
        arrive(k)
    for t in range(nz - 1):
        uz[t].wait_recv()
        sums = sums + fz[t]
    num, den_mine, den_other = sums[0:1], sums[1:2], sums[2:3]
    fsc = num / (jnp.sqrt(den_mine * den_other) + 1e-06)
    factor = step * (1.0 + fsc) / 2.0
    column = jnp.sum(eye(radii, F32) * factor, axis=1, keepdims=True)
    column = jnp.concatenate([column, column], axis=0)

    for copy, needed in pair_copies:
        if needed is None:
            copy.wait_recv()
        else:
            pl.when(needed)(copy.wait_recv)
    if bw % CHUNK == 0:
        for b in range(n_dom):
            out[:, b * bw:(b + 1) * bw] = (column * gall[b].astype(F32)).astype(BF16)
    else:
        fold = CHUNK // bw

        @pl.loop(0, lines // CHUNK)
        def _(c):
            whole = jnp.zeros((cols, CHUNK), F32)
            for u in range(fold):
                whole = whole + jnp.dot(gall[c * fold + u], placing(bw, u * bw), preferred_element_type=F32)
            out[:, pl.ds(pl.multiple_of(c * CHUNK, CHUNK), CHUNK)] = (column * whole).astype(BF16)

    for copy, needed in sends:
        if needed is None:
            copy.wait_send()
        else:
            pl.when(needed)(copy.wait_send)


def body(n_dom, n_slab, volume, images, tap_index, tap_weight, classes, shifts, defocus):
    slab_map, data = volume[0].T, images[0].T
    cols, lines = slab_map.shape
    rows = data.shape[1]
    depth = tap_index.shape[2]
    step = STEP_SCALE / math.sqrt(rows * n_dom * depth / lines)
    nz, bw = n_dom // 2, lines // n_dom
    nc, np_, nq = lines // CHUNK, n_slab - 1, lines // CHUNK // 4
    dma = pltpu.SemaphoreType.DMA
    vmem = pl.BlockSpec(memory_space=pltpu.VMEM)
    scratch = [
        pltpu.VMEM((cols, lines), F32),
        pltpu.VMEM((cols, rows), BF16),
        pltpu.VMEM(tap_index.shape[2:], jnp.int32),
        pltpu.VMEM(tap_weight.shape[2:], F32),
        pltpu.SMEM(classes.shape, jnp.int32),
        pltpu.SMEM(shifts.shape, jnp.int32),
        pltpu.SMEM(defocus.shape, F32),
        pltpu.VMEM((nc, cols, CHUNK), BF16),
        pltpu.VMEM((np_, nc, cols, CHUNK), BF16),
        pltpu.VMEM((16, rows), BF16),
        pltpu.VMEM((np_, 16, rows), BF16),
        pltpu.VMEM((lines, rows), BF16),
        pltpu.VMEM((lines, rows), BF16),
        pltpu.VMEM((cols, rows), F32),
        pltpu.VMEM((cols, rows), F32),
        pltpu.VMEM((cols, rows), F32),
        pltpu.VMEM((cols, rows), BF16),
        pltpu.VMEM((nz, cols, bw), F32),
        pltpu.VMEM((nz, cols, bw), BF16),
        pltpu.VMEM((nz, cols, bw), BF16),
        pltpu.VMEM((nz - 1, cols, bw), BF16),
        pltpu.VMEM((nz - 1, cols, bw), BF16),
        pltpu.VMEM((n_dom, cols, bw), BF16),
        pltpu.VMEM((cols, bw), BF16),
        pltpu.VMEM((cols, bw), BF16),
        pltpu.VMEM((3, 8, cols // 2), F32),
        pltpu.VMEM((np_, 8, cols // 2), F32),
        pltpu.VMEM((8, cols // 2), F32),
        pltpu.VMEM((nz - 1, 8, cols // 2), F32),
    ]
    for shape in (
        (np_,), (np_, 2 * nq), (np_, nq), (np_, nq), (nz, 2), (nz - 1, 2), (2, nz - 1, 2), (2, nz, 2), (1,), (np_,), (1,), (nz - 1,), (np_,)
    ):
        scratch += [dma(shape), dma(shape)]
    scratch.append(dma((7,)))
    change = pl.pallas_call(
        functools.partial(kernel, n_dom, n_slab, step),
        out_shape=jax.ShapeDtypeStruct((cols, lines), BF16),
        in_specs=[pl.BlockSpec(memory_space=pltpu.HBM)] * 7,
        out_specs=vmem,
        scratch_shapes=scratch,
        compiler_params=pltpu.CompilerParams(
            collective_id=0, has_side_effects=True, vmem_limit_bytes=60 * 1024 * 1024
        ),
    )(slab_map, data, tap_index[0, 0], tap_weight[0, 0], classes, shifts, defocus)
    return (slab_map - change.astype(F32)).T[None]


def solution(mesh):
    placed = (
        P("half", "slab", None),
        P("half", "dom", None),
        P("half", "slab", None, "dom"),
        P("half", "slab", None, "dom"),
        P("half", "dom"),
        P("half", None, "dom"),
        P(),
    )
    return jax.shard_map(
        functools.partial(body, mesh.shape["dom"], mesh.shape["slab"]),
        mesh=mesh, in_specs=placed, out_specs=P("half", "slab", None), check_vma=False,
    )
```
